256 devices in a mesh: dp: 16 (over y, x_hi, core), ctx: 16 (over x_lo, z).
Axes of the slice: x: 4 (x_hi: 2, x_lo: 2; x = x_hi * 2 + x_lo), y: 4, z: 8, core: 2. Of those that a mesh axis runs over, the one named last changes fastest.
Arguments:
- q_comp: bfloat16 [16, 4096, 640], P('dp', 'ctx'), may hold values from -6 to 6
- k_comp: bfloat16 [16, 4096, 128], P('dp', 'ctx'), may hold values from -6 to 6
- v_comp: bfloat16 [16, 4096, 128], P('dp', 'ctx'), may hold values from -6 to 6
- o_comp: bfloat16 [16, 4096, 640], P('dp', 'ctx'), may hold values from -6 to 6
- d_out: bfloat16 [16, 4096, 640], P('dp', 'ctx'), may hold values from -6 to 6
- k_prompt: bfloat16 [16, 6144, 128], P('dp', 'ctx'), may hold values from -12 to 12
- v_prompt: bfloat16 [16, 6144, 128], P('dp', 'ctx'), may hold values from -6 to 6
- kept_counts: int32 [16], P('dp'), may hold values from 8 to 16, as said below
- comp_len: int32 [16, 16], P('dp'), may hold values from 1 to 2, as said below
- owner_list: int32 [16, 16], P('dp'), may hold values from 0 to 15, as said below
Outputs:
- dq_comp: bfloat16 [16, 4096, 640], P('dp', 'ctx')
- dk_comp: bfloat16 [16, 4096, 128], P('dp', 'ctx')
- dv_comp: bfloat16 [16, 4096, 128], P('dp', 'ctx')
- dk_prompt: bfloat16 [16, 6144, 128], P('dp', 'ctx')
- dv_prompt: bfloat16 [16, 6144, 128], P('dp', 'ctx')
The draws below stay inside these ranges and needn't reach their ends.
Inputs may be any that keep to these rules, and one draw needn't show every extreme that they name: `kept_counts`: some prompt keeps 16. `comp_len`: entries of completions j >= kept_counts of a prompt are not used. `owner_list`: the kept completions of one prompt held by one ctx position take at most 2 blocks, and exactly 2 at some position.
All inputs are finite; a program needn't handle non-finite values.
Results may differ from the reference program's by a relative error of at most 0.018.
Values may be sent and summed in bfloat16 or wider, within the bound.
No kernel may reach another device: no remote copies, remote signals or barrier semaphores. Data moves between devices by JAX's collectives and lax.ppermute only.
A program may use at most 128 MiB of HBM per device.

```python
import jax
import jax.numpy as jnp
from jax import lax

D_HEAD = 128
GROUP = 5
BLOCK = 128
CBLK = 2
MAXC = 16
PROMPTS = 16
PROMPT = 6144
SLOTS = 2
CTOK = 4096
N_CTX = 16


def draw_q_comp(key, part):
    key = jax.random.fold_in(key, 11)
    array_shape = (PROMPTS, CTOK, GROUP * D_HEAD)
    values = 0.5 * jnp.clip(jax.random.normal(key, array_shape, jnp.float32), -4.0, 4.0)
    return values.astype(jnp.bfloat16)


def draw_k_prompt(key, part):
    key = jax.random.fold_in(key, 13)
    scale_key, noise_key = jax.random.split(key)
    array_shape = (PROMPTS, PROMPT, D_HEAD)
    row_scale = jnp.exp(jax.random.uniform(scale_key, (PROMPTS, PROMPT, 1), jnp.float32, jnp.log(0.4), jnp.log(4.0)))
    values = row_scale * jnp.clip(jax.random.normal(noise_key, array_shape, jnp.float32), -3.0, 3.0)
    return values.astype(jnp.bfloat16)


def draw_kept_counts(key, part):
    key = jax.random.fold_in(key, 3)
    prompt_ids = jnp.arange(PROMPTS, dtype=jnp.int32)
    base_count = MAXC // 2 + MAXC // 2 * prompt_ids // (PROMPTS - 1)
    jitter = jax.random.randint(key, (PROMPTS,), -1, 2)
    counts_drawn = jnp.clip(base_count + jitter, MAXC // 2, MAXC)
    return counts_drawn.at[PROMPTS - 1].set(MAXC).astype(jnp.int32)


def draw_comp_len(key, part):
    key = jax.random.fold_in(key, 5)
    prompt_ids = jnp.arange(PROMPTS)[:, None]
    chance = 0.05 + 0.9 * prompt_ids.astype(jnp.float32) / (PROMPTS - 1)
    favoured = jax.random.uniform(key, (PROMPTS, MAXC)) < chance
    lengths = jnp.where(favoured, CBLK, 1)
    numbers = jnp.arange(MAXC)[None, :]
    longest = (numbers == 0) | (prompt_ids == PROMPTS - 1) & (numbers % N_CTX == 0)
    return jnp.where(longest, CBLK, lengths).astype(jnp.int32)


def permute_cycle(subkey):
    return jax.random.permutation(subkey, N_CTX)


def draw_owner_list(key, part):
    key = jax.random.fold_in(key, 7)
    subkeys = jax.random.split(key, PROMPTS)
    orders = jax.vmap(permute_cycle)(subkeys)
    columns = jnp.arange(MAXC) % N_CTX
    return orders[:, columns].astype(jnp.int32)


def level_of(own_key, extent, shards, least, top_value):
    gain = 1.0
    for axis_at, blocks in shards:
        draws = jax.random.uniform(jax.random.fold_in(jax.random.fold_in(own_key, 6), axis_at), (blocks,), jnp.float32, least / len(shards), top_value / len(shards))
        gain = gain * jnp.repeat(jnp.exp(draws), extent[axis_at] // blocks).reshape((-1,) + (1,) * (len(extent) - 1 - axis_at))
    return gain


def scatter_about(own_key, shape, scale, reach, cuts=(), kind=jnp.bfloat16):
    result = scale * jax.random.normal(own_key, shape, jnp.float32)
    if cuts:
        result = result * level_of(own_key, shape, cuts, -0.22, 0.18)
    return jnp.clip(result, -reach, reach).astype(kind)


def setup_inputs(seed: int = 0) -> dict:
    key_list = jax.random.split(jax.random.key(seed), 11)
    q_comp = draw_q_comp(jax.random.fold_in(key_list[10], 71), 0)
    k_comp = scatter_about(key_list[1], (PROMPTS, CTOK, D_HEAD), 1.0, 6.0, ((0, 16), (1, 16)))
    v_comp = scatter_about(key_list[2], (PROMPTS, CTOK, D_HEAD), 1.0, 6.0, ((0, 16), (1, 16)))
    o_comp = scatter_about(key_list[3], (PROMPTS, CTOK, GROUP * D_HEAD), 1.0, 6.0, ((0, 16), (1, 16)))
    d_out = scatter_about(key_list[4], (PROMPTS, CTOK, GROUP * D_HEAD), 1.0, 6.0, ((0, 16), (1, 16)))
    k_prompt = draw_k_prompt(jax.random.fold_in(key_list[10], 71), 0)
    v_prompt = scatter_about(key_list[6], (PROMPTS, PROMPT, D_HEAD), 1.0, 6.0, ((0, 16), (1, 16)))
    kept_counts = draw_kept_counts(jax.random.fold_in(key_list[10], 71), 0)
    comp_len = draw_comp_len(jax.random.fold_in(key_list[10], 71), 0)
    owner_list = draw_owner_list(jax.random.fold_in(key_list[10], 71), 0)
    return dict(q_comp=q_comp, k_comp=k_comp, v_comp=v_comp, o_comp=o_comp, d_out=d_out, k_prompt=k_prompt, v_prompt=v_prompt, kept_counts=kept_counts, comp_len=comp_len, owner_list=owner_list)


masked_score = -1e30


def slot_layout(kept_now, len_row, owner_row, position, slot_count, block_len):
    numbers = jnp.arange(len_row.shape[0], dtype=jnp.int32)
    owned_here = ((owner_row == position) & (numbers < kept_now)).astype(jnp.int32)
    block_sizes = (len_row * owned_here).astype(jnp.int32)
    starts = (jnp.cumsum(block_sizes) - block_sizes).astype(jnp.int32)
    slot_ids = jnp.arange(slot_count, dtype=jnp.int32)[:, None]
    member = ((owned_here[None, :] > 0) & (slot_ids >= starts[None, :]) & (slot_ids < (starts + block_sizes)[None, :])).astype(jnp.int32)
    filled = jnp.sum(member, axis=1).astype(jnp.int32)
    comp_ids = jnp.where(filled > 0, jnp.sum(member * numbers[None, :], axis=1), -1).astype(jnp.int32)
    block_pos = jnp.sum(member * (slot_ids - starts[None, :]), axis=1).astype(jnp.int32)
    offsets = jnp.arange(block_len, dtype=jnp.int32)
    positions = (block_pos[:, None] * block_len + offsets[None, :]).reshape(-1).astype(jnp.int32)
    return jnp.repeat(comp_ids, block_len), positions, jnp.repeat(filled, block_len) > 0


def self_mask(comp_ids, positions, head_count):
    same_comp = (comp_ids[:, None] == comp_ids[None, :]) & (comp_ids[:, None] >= 0) & (positions[None, :] <= positions[:, None])
    return jnp.repeat(same_comp, head_count, axis=0)


def grads_block(queries, grad_rows, deltas, logsum, key_rows, value_rows, allowed):
    score_scale = key_rows.shape[1] ** -0.5
    scores = jnp.dot(queries, key_rows.T, preferred_element_type=jnp.float32) * score_scale
    if allowed is not None:
        scores = jnp.where(allowed, scores, masked_score)
    weights = jnp.exp(scores - logsum[:, None])
    weights_low = weights.astype(jnp.bfloat16)
    value_grad = jnp.dot(weights_low.T, grad_rows, preferred_element_type=jnp.float32)
    weight_grad = jnp.dot(grad_rows, value_rows.T, preferred_element_type=jnp.float32)
    score_grad = (weights * (weight_grad - deltas[:, None])).astype(jnp.bfloat16)
    query_grad = jnp.dot(score_grad, key_rows, preferred_element_type=jnp.float32)
    key_grad = jnp.dot(score_grad.T, queries, preferred_element_type=jnp.float32)
    return query_grad, key_grad, value_grad


def reference(q_comp, k_comp, v_comp, o_comp, d_out, k_prompt, v_prompt, kept_counts, comp_len, owner_list):
    feature_width = q_comp.shape[2]
    d_head = k_prompt.shape[2]
    head_count = feature_width // d_head
    row_count = SLOTS * BLOCK
    score_scale = d_head ** -0.5
    numbers = jnp.arange(MAXC, dtype=jnp.int32)
    used_blocks = jnp.where(numbers[None, :] < kept_counts[:, None], comp_len, 0)
    token_total = (jnp.sum(used_blocks) * BLOCK).astype(jnp.float32)
    factor = jnp.float32(PROMPTS * CTOK) / token_total

    def one_prompt(inputs):
        query_all, comp_keys_all, comp_values_all, output_all, dout_all, prompt_keys, prompt_values, kept_now, len_row, owner_row = inputs

        def one_position(running, position):
            key_acc, value_acc = running
            offset = (position * row_count).astype(jnp.int32)

            def take_rows(array):
                return lax.dynamic_slice_in_dim(array, offset, row_count, 0)

            comp_ids, positions, filled = slot_layout(kept_now, len_row, owner_row, position, SLOTS, BLOCK)
            queries = take_rows(query_all).reshape(row_count * head_count, d_head)
            grad_tok = (take_rows(dout_all).astype(jnp.float32) * factor * filled[:, None].astype(jnp.float32)).astype(jnp.bfloat16)
            grad_rows = grad_tok.reshape(row_count * head_count, d_head)
            out_rows = take_rows(output_all).reshape(row_count * head_count, d_head)
            deltas = jnp.sum(grad_rows.astype(jnp.float32) * out_rows.astype(jnp.float32), axis=1)
            comp_keys = take_rows(comp_keys_all)
            comp_values = take_rows(comp_values_all)
            allowed = self_mask(comp_ids, positions, head_count)
            scores_prompt = jnp.dot(queries, prompt_keys.T, preferred_element_type=jnp.float32) * score_scale
            scores_comp = jnp.where(allowed, jnp.dot(queries, comp_keys.T, preferred_element_type=jnp.float32) * score_scale, masked_score)
            top_rows = jnp.maximum(jnp.max(scores_prompt, axis=1), jnp.max(scores_comp, axis=1))
            totals = jnp.sum(jnp.exp(scores_prompt - top_rows[:, None]), axis=1) + jnp.sum(jnp.exp(scores_comp - top_rows[:, None]), axis=1)
            logsum = top_rows + jnp.log(totals)
            query_p, key_p, value_p = grads_block(queries, grad_rows, deltas, logsum, prompt_keys, prompt_values, None)
            query_c, key_c, value_c = grads_block(queries, grad_rows, deltas, logsum, comp_keys, comp_values, allowed)
            query_out = ((query_p + query_c) * score_scale).reshape(row_count, feature_width).astype(jnp.bfloat16)
            key_out = (key_c * score_scale).astype(jnp.bfloat16)
            value_out = value_c.astype(jnp.bfloat16)
            return (key_acc + key_p, value_acc + value_p), (query_out, key_out, value_out)

        zeros_keys = jnp.zeros((PROMPT, d_head), jnp.float32)
        (key_acc, value_acc), (query_out, key_out, value_out) = lax.scan(one_position, (zeros_keys, zeros_keys), jnp.arange(N_CTX, dtype=jnp.int32))
        return (query_out.reshape(CTOK, feature_width), key_out.reshape(CTOK, d_head), value_out.reshape(CTOK, d_head),
                (key_acc * score_scale).astype(jnp.bfloat16), value_acc.astype(jnp.bfloat16))

    dq_comp, dk_comp, dv_comp, dk_prompt, dv_prompt = lax.map(one_prompt, (q_comp, k_comp, v_comp, o_comp, d_out, k_prompt, v_prompt, kept_counts, comp_len, owner_list))
    return (dq_comp, dk_comp, dv_comp, dk_prompt, dv_prompt)
```

```python
import jax
import jax.numpy as jnp
from jax import lax
from jax.experimental import pallas as pl
from jax.experimental.pallas import tpu as pltpu
from jax.sharding import PartitionSpec as P

BLOCK = 128
LOG2E = 1.4426950408889634
masked_score = -1e30
f32 = jnp.float32
bf16 = jnp.bfloat16


def dg(a, b, ca, cb):
    return lax.dot_general(a, b, (((ca,), (cb,)), ((), ())), preferred_element_type=f32)


def call(kern, outs, ins, flops=0, smem=(), scratch=(), vmem=40, trans=0):
    total = sum(x.size * x.dtype.itemsize for x in ins) + sum(
        o.size * o.dtype.itemsize for o in outs
    )
    specs = [
        pl.BlockSpec(memory_space=pltpu.SMEM if i in smem else pltpu.VMEM) for i in range(len(ins))
    ]
    return pl.pallas_call(
        kern,
        out_shape=outs,
        in_specs=specs,
        out_specs=[pl.BlockSpec(memory_space=pltpu.VMEM)] * len(outs),
        scratch_shapes=list(scratch),
        compiler_params=pltpu.CompilerParams(vmem_limit_bytes=vmem * 2**20),
        cost_estimate=pl.CostEstimate(flops=int(flops), bytes_accessed=int(total), transcendentals=int(trans)),
    )(*ins)


def sds(shape, dtype=f32):
    return jax.ShapeDtypeStruct(shape, dtype)


def head(ref, h):
    return ref[:, h * 128 : (h + 1) * 128]


def stat_scores(scores, m_old, l_old):
    top = jnp.max(scores, axis=0, keepdims=True)
    if m_old is not None:
        top = jnp.maximum(top, m_old)
    total = jnp.sum(jnp.exp2(scores - top), axis=0, keepdims=True)
    if m_old is not None:
        total = total + l_old * jnp.exp2(m_old - top)
    return top, total


def causal(same, n):
    key = lax.broadcasted_iota(jnp.int32, (n, n), 0)
    row = lax.broadcasted_iota(jnp.int32, (n, n), 1)
    same_block = (key // BLOCK) == (row // BLOCK)
    return (key <= row) & (same_block | (same > 0))


def first_kernel(heads, c):
    def kern(info, q_ref, d_ref, o_ref, k_ref, kc_ref, g_ref, st_ref):
        rows = q_ref.shape[0]
        slot = lax.broadcasted_iota(jnp.int32, (rows, 128), 0) // BLOCK
        filled = slot < info[0]
        mask = causal(info[1], rows)
        k = k_ref[...]
        kc = kc_ref[...]
        st_ref[...] = jnp.zeros_like(st_ref)
        for h in range(heads):
            q = head(q_ref, h)
            g = jnp.where(filled, head(d_ref, h), jnp.zeros((), bf16))
            g_ref[:, h * 128 : (h + 1) * 128] = g
            prod = g.astype(f32) * head(o_ref, h).astype(f32)
            st_ref[32 + h : 33 + h, :] = jnp.sum(jnp.transpose(prod), axis=0, keepdims=True)
            top, total = stat_scores(dg(k, q, 1, 1) * c, None, None)
            comp = jnp.where(mask, dg(kc, q, 1, 1) * c, masked_score)
            top, total = stat_scores(comp, top, total)
            st_ref[h : h + 1, :] = top
            st_ref[8 + h : 9 + h, :] = total

    return kern


def stat_kernel(heads, c, n_keys, first):
    def kern(qo_ref, qp_ref, st_in, *refs):
        k_refs, st_ref = refs[:-1], refs[-1]
        st_ref[...] = st_in[...]
        for a, q_ref in enumerate((qo_ref, qp_ref)):
            base = 16 * a
            for h in range(heads):
                q = head(q_ref, h)
                if first and a == 1:
                    top, total = None, None
                else:
                    top = st_ref[base + h : base + h + 1, :]
                    total = st_ref[base + 8 + h : base + 9 + h, :]
                used = k_refs[1:] if first and a == 0 else k_refs
                for k_ref in used:
                    top, total = stat_scores(dg(k_ref[...], q, 1, 1) * c, top, total)
                st_ref[base + h : base + h + 1, :] = top
                st_ref[base + 8 + h : base + 9 + h, :] = total

    return kern


def merged_lse(m_one, l_one, m_two, l_two):
    top = jnp.maximum(m_one, m_two)
    return top + jnp.log2(l_one * jnp.exp2(m_one - top) + l_two * jnp.exp2(m_two - top))


def lse_of(st, rc, a, h):
    b = 16 - 16 * a
    o = 16 * a
    return merged_lse(
        st[o + h : o + h + 1, :],
        st[o + 8 + h : o + 9 + h, :],
        rc[b + h : b + h + 1, :],
        rc[b + 8 + h : b + 9 + h, :],
    )


def grad_kernel(heads, c, n_sets, has_in, last):
    def kern(qo, qp, go, gp, st, rc, *refs):
        k_refs = refs[:n_sets]
        v_refs = refs[n_sets : 2 * n_sets]
        rest = refs[2 * n_sets :]
        if has_in:
            dq_in, rest = rest[0], rest[1:]
        if last:
            kv_out, dq_out, dqp_out, dk_s, dv_s = rest
        else:
            kv_out, dq_out, dk_s, dv_s = rest
        k = jnp.concatenate([r[...] for r in k_refs], axis=0) if n_sets > 1 else k_refs[0][...]
        v = jnp.concatenate([r[...] for r in v_refs], axis=0) if n_sets > 1 else v_refs[0][...]
        kt = jnp.transpose(k)
        for a in range(2):
            for h in range(heads):
                q = head((qo, qp)[a], h)
                g = head((go, gp)[a], h)
                lse = lse_of(st, rc, a, h)
                delta = (st, rc)[a][32 + h : 33 + h, :]
                p = jnp.exp2(dg(k, q, 1, 1) * c - lse)
                ds = (p * (dg(v, g, 1, 1) - delta)).astype(bf16)
                dv = dg(p.astype(bf16), g, 1, 0)
                dk = dg(ds, q, 1, 0)
                if a == 0 and h == 0:
                    dk_s[...] = dk
                    dv_s[...] = dv
                else:
                    dk_s[...] += dk
                    dv_s[...] += dv
                i = a * heads + h
                dq = dg(kt, ds, 1, 0)
                if has_in:
                    dq = dq + dq_in[i]
                if last and a == 1:
                    dqp_out[h] = dq.astype(bf16)
                else:
                    dq_out[i] = dq
        kv_out[:, :128] = dk_s[...].astype(kv_out.dtype)
        kv_out[:, 128:] = dv_s[...].astype(kv_out.dtype)

    return kern


def comp_kernel(heads, c):
    def kern(info, q_ref, g_ref, st, rc, kc_ref, vc_ref, dq_in, kv_out, dq_out):
        mask = causal(info[1], q_ref.shape[0])
        k = kc_ref[...]
        v = vc_ref[...]
        kt = jnp.transpose(k)
        dk_sum = dv_sum = None
        for h in range(heads):
            q = head(q_ref, h)
            g = head(g_ref, h)
            lse = lse_of(st, rc, 0, h)
            delta = st[32 + h : 33 + h, :]
            s = jnp.where(mask, dg(k, q, 1, 1) * c, masked_score)
            p = jnp.exp2(s - lse)
            ds = (p * (dg(v, g, 1, 1) - delta)).astype(bf16)
            dv = dg(p.astype(bf16), g, 1, 0)
            dk = dg(ds, q, 1, 0)
            dk_sum = dk if h == 0 else dk_sum + dk
            dv_sum = dv if h == 0 else dv_sum + dv
            dq_out[h] = dq_in[h] + dg(kt, ds, 1, 0)
        kv_out[:, :128] = dk_sum
        kv_out[:, 128:] = dv_sum

    return kern


def middle_kernel(n):
    def kern(own, three, two, down, up, keep):
        down[...] = (own[:n] + three[:n].astype(f32) + two[:n].astype(f32)).astype(bf16)
        keep[...] = own[n : 2 * n] + three[n : 2 * n].astype(f32) + two[n:].astype(f32)
        up[...] = (own[2 * n :] + three[2 * n :].astype(f32)).astype(bf16)

    return kern


def end_kernel(heads, scale):
    def kern(fac, keep, one, two, ckv, dq_own, dq_rc, dq, dkc, dvc, dkp, dvp):
        factor = fac[0]
        kv = keep[...] + one[...].astype(f32) + two[...].astype(f32)
        dkp[...] = (kv[:, :128] * (scale * factor)).astype(bf16)
        dvp[...] = (kv[:, 128:] * factor).astype(bf16)
        dkc[...] = (ckv[:, :128] * (scale * factor)).astype(bf16)
        dvc[...] = (ckv[:, 128:] * factor).astype(bf16)
        for h in range(heads):
            t = (dq_own[h] + dq_rc[h].astype(f32)) * (scale * factor)
            dq[:, h * 128 : (h + 1) * 128] = jnp.transpose(t).astype(bf16)

    return kern


def along_z(value, step, n_dp, n_z):
    pairs = []
    for d in range(n_dp):
        turn = step if d % 2 == 0 else -step
        for x in range(2):
            for z in range(n_z):
                source = (d * 2 + x) * n_z + z
                pairs.append((source, (d * 2 + x) * n_z + (z + turn) % n_z))
    return lax.ppermute(value, ("dp", "ctx"), pairs)


def across_x(value, n_z):
    return lax.ppermute(value, "ctx", [(i, (i + n_z) % (2 * n_z)) for i in range(2 * n_z)])


def per_device(
    q_comp, k_comp, v_comp, o_comp, d_out, k_prompt, v_prompt, kept_counts, comp_len, owner_list
):
    n_ctx = lax.axis_size("ctx")
    n_dp = lax.axis_size("dp")
    n_z = n_ctx // 2
    position = lax.axis_index("ctx")
    q, kc, vc = q_comp[0], k_comp[0], v_comp[0]
    o, d, k, v = o_comp[0], d_out[0], k_prompt[0], v_prompt[0]
    rows, width = q.shape
    n_keys, d_head = k.shape
    heads = width // d_head
    scale = d_head ** (-0.5)
    c = scale * LOG2E
    pair_flops = 2 * rows * heads * d_head

    numbers = jnp.arange(comp_len.shape[1], dtype=jnp.int32)
    used = jnp.where(numbers < kept_counts[0], comp_len[0], 0)
    owned = jnp.where(owner_list[0] == position, used, 0)
    info = jnp.stack([jnp.sum(owned), jnp.max(owned) - 1])
    token_total = lax.psum((jnp.sum(used) * BLOCK).astype(f32), "dp")
    factor = f32(n_dp * n_ctx * rows) / token_total

    def zmove(value, step):
        return along_z(value, step, n_dp, n_z)

    k_dn = zmove(k, 3)
    k_up = zmove(k, -3)
    qp = across_x(q, n_z)
    g, st = call(
        first_kernel(heads, c),
        [sds((rows, width), bf16), sds((40, rows))],
        [info, q, d, o, k, kc],
        flops=pair_flops * (n_keys + rows) * 2,
        smem=(0,),
    )
    gp = across_x(g, n_z)
    v_dn = zmove(v, 3)
    v_up = zmove(v, -3)
    k_three = zmove(jnp.concatenate([k_dn, k, k_up], axis=0), 1)
    k_two = zmove(jnp.concatenate([k_dn, k], axis=0), -1)
    st = call(
        stat_kernel(heads, c, n_keys, True),
        [sds((40, rows))],
        [q, qp, st, k, k_dn, k_up],
        flops=pair_flops * n_keys * 5 * 2,
    )[0]
    v_three = zmove(jnp.concatenate([v_dn, v, v_up], axis=0), 1)
    v_two = zmove(jnp.concatenate([v_dn, v], axis=0), -1)
    st = call(
        stat_kernel(heads, c, n_keys, False),
        [sds((40, rows))],
        [q, qp, st, k_two],
        flops=pair_flops * n_keys * 4 * 2,
    )[0]
    st = call(
        stat_kernel(heads, c, n_keys, False),
        [sds((40, rows))],
        [q, qp, st, k_three],
        flops=pair_flops * n_keys * 6 * 2,
    )[0]
    rc = across_x(st, n_z)

    def grads(k_sets, v_sets, dq_in, last, out_type):
        total = sum(x.shape[0] for x in k_sets)
        outs = [sds((total, 2 * d_head), out_type)]
        outs.append(sds((heads if last else 2 * heads, d_head, rows)))
        if last:
            outs.append(sds((heads, d_head, rows), bf16))
        ins = [q, qp, g, gp, st, rc, *k_sets, *v_sets]
        if dq_in is not None:
            ins.append(dq_in)
        return call(
            grad_kernel(heads, c, len(k_sets), dq_in is not None, last),
            outs,
            ins,
            flops=pair_flops * 2 * total * 5 * 2,
            scratch=[pltpu.VMEM((total, d_head), f32)] * 2,
        )

    kv_three, dq = grads([k_three], [v_three], None, False, bf16)
    in_three = zmove(kv_three, -1)
    kv_two, dq = grads([k_two], [v_two], dq, False, bf16)
    in_two = zmove(kv_two, 1)
    kv_own, dq, dqp = grads([k_dn, k, k_up], [v_dn, v, v_up], dq, True, f32)
    dq_rc = across_x(dqp, n_z)
    ckv, dq = call(
        comp_kernel(heads, c),
        [sds((rows, 2 * d_head)), sds((heads, d_head, rows))],
        [info, q, g, st, rc, kc, vc, dq],
        flops=pair_flops * rows * 5 * 2,
        smem=(0,),
    )
    down, up, keep = call(
        middle_kernel(n_keys),
        [sds((n_keys, 2 * d_head), bf16), sds((n_keys, 2 * d_head), bf16), sds((n_keys, 2 * d_head))],
        [kv_own, in_three, in_two],
    )
    from_up = zmove(down, -3)
    from_dn = zmove(up, 3)
    outs = call(
        end_kernel(heads, scale),
        [
            sds((rows, width), bf16),
            sds((rows, d_head), bf16),
            sds((rows, d_head), bf16),
            sds((n_keys, d_head), bf16),
            sds((n_keys, d_head), bf16),
        ],
        [factor.reshape(1), keep, from_up, from_dn, ckv, dq, dq_rc],
        smem=(0,),
    )
    return tuple(x[None] for x in outs)


def solution(mesh):
    split = P("dp", "ctx", None)
    return jax.shard_map(
        per_device,
        mesh=mesh,
        in_specs=(split,) * 7 + (P("dp"), P("dp", None), P("dp", None)),
        out_specs=(split,) * 5,
        check_vma=False,
    )
```

```python
import jax
import jax.numpy as jnp
from jax import lax
from jax.experimental import pallas as pl
from jax.experimental.pallas import tpu as pltpu
from jax.sharding import PartitionSpec as P

BLOCK = 128
EXTRA = 16
LOG2E = 1.4426950408889634
masked_score = -1e30
f32 = jnp.float32
bf16 = jnp.bfloat16


def dg(a, b, ca, cb):
    return lax.dot_general(a, b, (((ca,), (cb,)), ((), ())), preferred_element_type=f32)


def call(kern, outs, ins, flops=0, smem=(), hbm=(), scratch=(), vmem=40):
    total = sum(x.size * x.dtype.itemsize for x in ins) + sum(
        o.size * o.dtype.itemsize for o in outs
    )
    spaces = {**{i: pltpu.SMEM for i in smem}, **{i: pltpu.HBM for i in hbm}}
    specs = [pl.BlockSpec(memory_space=spaces.get(i, pltpu.VMEM)) for i in range(len(ins))]
    return pl.pallas_call(
        kern,
        out_shape=outs,
        in_specs=specs,
        out_specs=[pl.BlockSpec(memory_space=pltpu.VMEM)] * len(outs),
        scratch_shapes=list(scratch),
        compiler_params=pltpu.CompilerParams(vmem_limit_bytes=vmem * 2**20),
        cost_estimate=pl.CostEstimate(flops=int(flops), bytes_accessed=1, transcendentals=0),
    )(*ins)


def sds(shape, dtype=f32):
    return jax.ShapeDtypeStruct(shape, dtype)


def head(ref, h):
    return ref[:, h * 128 : (h + 1) * 128]


def stat_scores(scores, m_old, l_old):
    top = jnp.max(scores, axis=0, keepdims=True)
    if m_old is not None:
        top = jnp.maximum(top, m_old)
    total = jnp.sum(jnp.exp2(scores - top), axis=0, keepdims=True)
    if m_old is not None:
        total = total + l_old * jnp.exp2(m_old - top)
    return top, total


def run_info(kept, lens, owners, position):
    blocks = same = jnp.int32(0)
    for j in range(lens.shape[1]):
        n = jnp.where(j < kept[0], lens[0, j], 0)
        mine = jnp.where(owners[0, j] == position, n, 0)
        blocks = blocks + mine
        same = jnp.maximum(same, mine - 1)
    return blocks, same


def causal(same, n):
    key = lax.broadcasted_iota(jnp.int32, (n, n), 0)
    row = lax.broadcasted_iota(jnp.int32, (n, n), 1)
    same_block = (key // BLOCK) == (row // BLOCK)
    return (key <= row) & (same_block | (same > 0))


def first_kernel(heads, c):
    def kern(
        kept_any, lens_any, owners_any, k_any, q_any, kc_any, v_any, d_any, o_any, st_ref, v_ref,
        kept, lens, owners, k_ref, q_ref, kc_ref, d_ref, o_ref, sems,
    ):
        pairs = (
            (kept_any, kept), (lens_any, lens), (owners_any, owners), (k_any, k_ref),
            (q_any, q_ref), (kc_any, kc_ref), (v_any, v_ref), (d_any, d_ref), (o_any, o_ref),
        )
        copies = [pltpu.make_async_copy(x, y, sems.at[i]) for i, (x, y) in enumerate(pairs)]
        for copy in copies:
            copy.start()
        for copy in copies[:3]:
            copy.wait()
        rows = q_ref.shape[0]
        blocks, same = run_info(kept, lens, owners, lax.axis_index("ctx"))
        empty = lax.broadcasted_iota(jnp.int32, (1, rows), 1) // BLOCK >= blocks
        mask = causal(same, rows)
        st_ref[...] = jnp.zeros_like(st_ref)
        st_ref[38:39, :] = jnp.full((1, rows), same.astype(f32))
        for copy in copies[3:6]:
            copy.wait()
        k = k_ref[...]
        kc = kc_ref[...]
        for h in range(heads):
            q = head(q_ref, h)
            top, total = stat_scores(dg(k, q, 1, 1) * c, None, None)
            comp = jnp.where(mask, dg(kc, q, 1, 1) * c, masked_score)
            top, total = stat_scores(comp, top, total)
            st_ref[h : h + 1, :] = jnp.where(empty, -masked_score, top)
            st_ref[8 + h : 9 + h, :] = jnp.where(empty, 1.0, total)
        for copy in copies[6:]:
            copy.wait()
        for h in range(heads):
            prod = head(d_ref, h).astype(f32) * head(o_ref, h).astype(f32)
            st_ref[32 + h : 33 + h, :] = jnp.sum(jnp.transpose(prod), axis=0, keepdims=True)

    return kern


def stat_kernel(heads, c, sides, counted=False):
    def kern(*refs):
        q_refs, refs = refs[: len(sides)], refs[len(sides) :]
        st_in, refs = refs[0], refs[1:]
        k_refs, st_ref = refs[:-1], refs[-1]
        st_ref[...] = st_in[...]
        if counted:
            cnt, k_refs = k_refs[0], k_refs[1:]
            row = cnt[0:1, :]
            st_ref[37:38, :] = jnp.concatenate([row] * (st_ref.shape[1] // 128), axis=1)
        for q_ref, (base, begun) in zip(q_refs, sides):
            for h in range(heads):
                q = head(q_ref, h)
                top = total = None
                if begun:
                    top = st_ref[base + h : base + h + 1, :]
                    total = st_ref[base + 8 + h : base + 9 + h, :]
                for k_ref in k_refs:
                    top, total = stat_scores(dg(k_ref[...], q, 1, 1) * c, top, total)
                st_ref[base + h : base + h + 1, :] = top
                st_ref[base + 8 + h : base + 9 + h, :] = total

    return kern


def join_kernel(dn, own, up, unused, near, pair):
    n = own.shape[0]
    for i, ref in enumerate((dn, own, up)):
        near[i * n : (i + 1) * n, :] = ref[...]
        if i < 2:
            pair[i * n : (i + 1) * n, :] = ref[...]


def merged_lse(m_one, l_one, m_two, l_two):
    top = jnp.maximum(m_one, m_two)
    return top + jnp.log2(l_one * jnp.exp2(m_one - top) + l_two * jnp.exp2(m_two - top))


def lse_of(st, rc, a, h):
    b = 16 - 16 * a
    o = 16 * a
    return merged_lse(
        st[o + h : o + h + 1, :],
        st[o + 8 + h : o + 9 + h, :],
        rc[b + h : b + h + 1, :],
        rc[b + 8 + h : b + 9 + h, :],
    )


def grad_kernel(heads, c, n_sets, n_tokens, n_keys, has_in, last):
    def kern(qo, qp, go, gp, st, rc, *refs):
        k_refs = refs[:n_sets]
        v_refs = refs[n_sets : 2 * n_sets]
        rest = refs[2 * n_sets + n_tokens :]
        if has_in:
            dq_in, rest = rest[0], rest[1:]
        if last:
            kv_out, dq_out, dqp_out, dk_s, dv_s = rest
        else:
            kv_out, dq_out, dk_s, dv_s = rest
        k = jnp.concatenate([r[...] for r in k_refs], axis=0) if n_sets > 1 else k_refs[0][...]
        v = jnp.concatenate([r[...] for r in v_refs], axis=0) if n_sets > 1 else v_refs[0][...]
        kt = jnp.transpose(k)
        for a in range(2):
            for h in range(heads):
                q = head((qo, qp)[a], h)
                g = head((go, gp)[a], h)
                lse = lse_of(st, rc, a, h)
                delta = (st, rc)[a][32 + h : 33 + h, :]
                p = jnp.exp2(dg(k, q, 1, 1) * c - lse)
                ds = (p * (dg(v, g, 1, 1) - delta)).astype(bf16)
                dv = dg(p.astype(bf16), g, 1, 0)
                dk = dg(ds, q, 1, 0)
                if a == 0 and h == 0:
                    dk_s[...] = dk
                    dv_s[...] = dv
                else:
                    dk_s[...] += dk
                    dv_s[...] += dv
                i = a * heads + h
                dq = dg(kt, ds, 1, 0)
                if has_in:
                    dq = dq + dq_in[i]
                if last and a == 1:
                    dqp_out[h] = dq.astype(bf16)
                else:
                    dq_out[i] = dq
        count = st[37:38, :] + rc[37:38, :]
        step = n_keys + EXTRA
        for b in range(k.shape[0] // n_keys):
            part = pl.ds(b * n_keys, n_keys)
            kv_out[b * step : b * step + n_keys, :128] = dk_s[part, :].astype(kv_out.dtype)
            kv_out[b * step : b * step + n_keys, 128:] = dv_s[part, :].astype(kv_out.dtype)
            kv_out[b * step + n_keys : (b + 1) * step, :] = jnp.broadcast_to(
                count, (EXTRA, kv_out.shape[1])
            ).astype(kv_out.dtype)

    return kern


def comp_kernel(heads, c):
    def kern(q_ref, g_ref, st, rc, kc_ref, vc_ref, dq_in, kv_out, dq_out):
        mask = causal(st[38:39, :], q_ref.shape[0])
        k = kc_ref[...]
        v = vc_ref[...]
        kt = jnp.transpose(k)
        dk_sum = dv_sum = None
        for h in range(heads):
            q = head(q_ref, h)
            g = head(g_ref, h)
            lse = lse_of(st, rc, 0, h)
            delta = st[32 + h : 33 + h, :]
            s = jnp.where(mask, dg(k, q, 1, 1) * c, masked_score)
            p = jnp.exp2(s - lse)
            ds = (p * (dg(v, g, 1, 1) - delta)).astype(bf16)
            dv = dg(p.astype(bf16), g, 1, 0)
            dk = dg(ds, q, 1, 0)
            dk_sum = dk if h == 0 else dk_sum + dk
            dv_sum = dv if h == 0 else dv_sum + dv
            dq_out[h] = dq_in[h] + dg(kt, ds, 1, 0)
        kv_out[:, :128] = dk_sum
        kv_out[:, 128:] = dv_sum

    return kern


def middle_kernel(n):
    def kern(own, three, two, down, up, keep):
        down[...] = (own[:n] + three[:n].astype(f32) + two[:n].astype(f32)).astype(bf16)
        keep[...] = own[n : 2 * n] + three[n : 2 * n].astype(f32) + two[n:].astype(f32)
        up[...] = (own[2 * n :] + three[2 * n :].astype(f32)).astype(bf16)

    return kern


def end_kernel(heads, scale, n_keys, all_slots):
    def kern(keep, one, two, ckv, dq_own, dq_rc, dq, dkc, dvc, dkp, dvp):
        kv = keep[...] + one[...].astype(f32) + two[...].astype(f32)
        factor = (all_slots / (BLOCK * kv[n_keys : n_keys + 1, :]))[:, :128]
        both = factor * scale
        dkp[...] = (kv[:n_keys, :128] * both).astype(bf16)
        dvp[...] = (kv[:n_keys, 128:] * factor).astype(bf16)
        dkc[...] = (ckv[:, :128] * both).astype(bf16)
        dvc[...] = (ckv[:, 128:] * factor).astype(bf16)
        for h in range(heads):
            t = jnp.transpose(dq_own[h] + dq_rc[h].astype(f32))
            dq[:, h * 128 : (h + 1) * 128] = (t * both).astype(bf16)

    return kern


def along_z(value, step, n_dp, n_z):
    pairs = []
    for d in range(n_dp):
        turn = step if d % 2 == 0 else -step
        for x in range(2):
            for z in range(n_z):
                source = (d * 2 + x) * n_z + z
                pairs.append((source, (d * 2 + x) * n_z + (z + turn) % n_z))
    return lax.ppermute(value, ("dp", "ctx"), pairs)


def across_x(value, n_z):
    return lax.ppermute(value, "ctx", [(i, (i + n_z) % (2 * n_z)) for i in range(2 * n_z)])


def per_device(
    q_comp, k_comp, v_comp, o_comp, d_out, k_prompt, v_prompt, kept_counts, comp_len, owner_list
):
    n_ctx = lax.axis_size("ctx")
    n_dp = lax.axis_size("dp")
    n_z = n_ctx // 2
    position = lax.axis_index("ctx")
    q, kc, vc = q_comp[0], k_comp[0], v_comp[0]
    o, d, k, v = o_comp[0], d_out[0], k_prompt[0], v_prompt[0]
    rows, width = q.shape
    n_keys, d_head = k.shape
    heads = width // d_head
    scale = d_head ** (-0.5)
    c = scale * LOG2E
    pair_flops = 2 * rows * heads * d_head

    lists = [kept_counts, comp_len, owner_list]

    def zmove(value, step):
        return along_z(value, step, n_dp, n_z)

    def after(value, *others):
        return lax.optimization_barrier((value, *others))[0]

    numbers = jnp.arange(comp_len.shape[1], dtype=jnp.int32)
    used = jnp.where(numbers < kept_counts[0], comp_len[0], 0)
    cnt = lax.ppermute(
        jnp.full((8, 128), jnp.sum(used).astype(f32)),
        ("dp", "ctx"),
        [(e * n_ctx + x, (e - x) % n_dp * n_ctx + x) for e in range(n_dp) for x in range(n_ctx)],
    )
    k_dn = zmove(k, 3)
    k_up = zmove(k, -3)
    qp = across_x(q, n_z)
    st, v_late = call(
        first_kernel(heads, c),
        [sds((40, rows)), sds((n_keys, d_head), bf16)],
        [*lists, k, q, kc, v, d, o],
        flops=pair_flops * (n_keys + rows) * 2,
        hbm=range(9),
        vmem=62,
        scratch=[pltpu.SMEM(x.shape, jnp.int32) for x in lists]
        + [pltpu.VMEM(x.shape, bf16) for x in (k, q, kc, d, o)]
        + [pltpu.SemaphoreType.DMA((9,))],
    )
    v_dn = zmove(v_late, 3)
    v_up = zmove(v_late, -3)
    gp = across_x(after(d, k_up, st), n_z)
    def joined(dn, own, up, token):
        return call(
            join_kernel,
            [sds((3 * n_keys, d_head), bf16), sds((2 * n_keys, d_head), bf16)],
            [dn, own, up, token],
        )

    k_near, k_pair = joined(k_dn, k, k_up, st)
    k_three = zmove(k_near, 1)
    k_two = zmove(k_pair, -1)

    def stats(q_list, st, k_list, sides, counted=False):
        return call(
            stat_kernel(heads, c, sides, counted),
            [sds((40, rows))],
            [*q_list, st, *k_list],
            flops=pair_flops * sum(x.shape[0] for x in k_list) * len(q_list) * 2,
        )[0]

    own, partner = (0, True), (16, True)
    st = stats([q], st, [k_dn, k_up], [own])
    st = stats([qp], st, [k, k_dn, k_up], [(16, False)])
    v_near, v_pair = joined(v_dn, v, v_up, st)
    v_three = zmove(v_near, 1)
    v_two = zmove(v_pair, -1)
    st = stats([q, qp], st, [cnt, k_two], [own, partner], True)
    st = stats([q, qp], st, [k_three], [own, partner])
    rc = across_x(st, n_z)

    def grads(k_sets, v_sets, dq_in, last, out_type, tokens=()):
        total = sum(x.shape[0] for x in k_sets)
        long = total // n_keys * (n_keys + EXTRA)
        outs = [sds((long, 2 * d_head), out_type)]
        outs.append(sds((heads if last else 2 * heads, d_head, rows)))
        if last:
            outs.append(sds((heads, d_head, rows), bf16))
        ins = [q, qp, d, gp, st, rc, *k_sets, *v_sets, *tokens]
        if dq_in is not None:
            ins.append(dq_in)
        return call(
            grad_kernel(heads, c, len(k_sets), len(tokens), n_keys, dq_in is not None, last),
            outs,
            ins,
            scratch=[pltpu.VMEM((total, d_head), f32)] * 2,
        )

    kv_three, dq = grads([k_three], [v_three], None, False, bf16, [v_two])
    in_three = zmove(kv_three, -1)
    kv_two, dq = grads([k_two], [v_two], dq, False, bf16)
    in_two = zmove(kv_two, 1)
    kv_own, dq, dqp = grads([k_near], [v_near], dq, True, f32)
    block = (n_keys + EXTRA, 2 * d_head)
    down, up, keep = call(
        middle_kernel(block[0]),
        [sds(block, bf16), sds(block, bf16), sds(block)],
        [kv_own, in_three, in_two],
    )
    from_up = zmove(down, -3)
    from_dn = zmove(up, 3)
    dq_rc = across_x(dqp, n_z)
    ckv, dq = call(
        comp_kernel(heads, c),
        [sds((rows, 2 * d_head)), sds((heads, d_head, rows))],
        [q, d, st, rc, kc, vc, dq],
        flops=pair_flops * rows * 5 * 2,
    )
    outs = call(
        end_kernel(heads, scale, n_keys, float(n_dp * n_ctx * rows)),
        [
            sds((rows, width), bf16),
            sds((rows, d_head), bf16),
            sds((rows, d_head), bf16),
            sds((n_keys, d_head), bf16),
            sds((n_keys, d_head), bf16),
        ],
        [keep, from_up, from_dn, ckv, dq, dq_rc],
    )
    return tuple(x[None] for x in outs)


def solution(mesh):
    split = P("dp", "ctx", None)
    return jax.shard_map(
        per_device,
        mesh=mesh,
        in_specs=(split,) * 7 + (P("dp"), P("dp", None), P("dp", None)),
        out_specs=(split,) * 5,
        check_vma=False,
    )
```

```python
import jax
import jax.numpy as jnp
from jax import lax
from jax.experimental import pallas as pl
from jax.experimental.pallas import tpu as pltpu
from jax.sharding import PartitionSpec as P

BLOCK = 128
EXTRA = 16
LOG2E = 1.4426950408889634
masked_score = -1e30
f32 = jnp.float32
bf16 = jnp.bfloat16


def dg(a, b, ca, cb):
    return lax.dot_general(a, b, (((ca,), (cb,)), ((), ())), preferred_element_type=f32)


def call(kern, outs, ins, flops=0, smem=(), hbm=(), scratch=(), vmem=24):
    total = sum(x.size * x.dtype.itemsize for x in ins) + sum(
        o.size * o.dtype.itemsize for o in outs
    )
    spaces = {**{i: pltpu.SMEM for i in smem}, **{i: pltpu.HBM for i in hbm}}
    specs = [pl.BlockSpec(memory_space=spaces.get(i, pltpu.VMEM)) for i in range(len(ins))]
    return pl.pallas_call(
        kern,
        out_shape=outs,
        in_specs=specs,
        out_specs=[pl.BlockSpec(memory_space=pltpu.VMEM)] * len(outs),
        scratch_shapes=list(scratch),
        compiler_params=pltpu.CompilerParams(vmem_limit_bytes=vmem * 2**20),
        cost_estimate=pl.CostEstimate(flops=int(flops), bytes_accessed=1, transcendentals=0),
    )(*ins)


def sds(shape, dtype=f32):
    return jax.ShapeDtypeStruct(shape, dtype)


def head(ref, h):
    return ref[:, h * 128 : (h + 1) * 128]


def run_info(kept, lens, owners, position):
    blocks = same = jnp.int32(0)
    for j in range(lens.shape[1]):
        n = jnp.where(j < kept[0], lens[0, j], 0)
        mine = jnp.where(owners[0, j] == position, n, 0)
        blocks = blocks + mine
        same = jnp.maximum(same, mine - 1)
    return blocks, same


def causal(same, n):
    key = lax.broadcasted_iota(jnp.int32, (n, n), 0)
    row = lax.broadcasted_iota(jnp.int32, (n, n), 1)
    same_block = (key // BLOCK) == (row // BLOCK)
    return (key <= row) & (same_block | (same > 0))


def pack_kernel(k_any, v_any, kv_ref, sems):
    width = k_any.shape[1]
    one = pltpu.make_async_copy(k_any, kv_ref.at[:, :width], sems.at[0])
    two = pltpu.make_async_copy(v_any, kv_ref.at[:, width:], sems.at[1])
    one.start()
    two.start()
    one.wait()
    two.wait()


def first_kernel(heads, c):
    def kern(
        kept_any, lens_any, owners_any, q_any, kc_any, d_any, o_any, st_ref,
        kept, lens, owners, q_ref, kc_ref, d_ref, o_ref, sems,
    ):
        pairs = (
            (kept_any, kept), (lens_any, lens), (owners_any, owners),
            (q_any, q_ref), (kc_any, kc_ref), (d_any, d_ref), (o_any, o_ref),
        )
        copies = [pltpu.make_async_copy(x, y, sems.at[i]) for i, (x, y) in enumerate(pairs)]
        for copy in copies:
            copy.start()
        for copy in copies[:3]:
            copy.wait()
        rows = q_ref.shape[0]
        blocks, same = run_info(kept, lens, owners, lax.axis_index("ctx"))
        empty = lax.broadcasted_iota(jnp.int32, (1, rows), 1) // BLOCK >= blocks
        mask = causal(same, rows)
        st_ref[...] = jnp.zeros_like(st_ref)
        st_ref[38:39, :] = jnp.full((1, rows), same.astype(f32))
        for copy in copies[3:5]:
            copy.wait()
        kc = kc_ref[...]
        for h in range(heads):
            q = head(q_ref, h)
            comp = jnp.where(mask, dg(kc, q, 1, 1) * c, masked_score)
            top = jnp.max(comp, axis=0, keepdims=True)
            total = jnp.sum(jnp.exp2(comp - top), axis=0, keepdims=True)
            st_ref[h : h + 1, :] = jnp.where(empty, -masked_score, top)
            st_ref[8 + h : 9 + h, :] = jnp.where(empty, 1.0, total)
        for copy in copies[5:]:
            copy.wait()
        for h in range(heads):
            prod = head(d_ref, h).astype(f32) * head(o_ref, h).astype(f32)
            st_ref[32 + h : 33 + h, :] = jnp.sum(jnp.transpose(prod), axis=0, keepdims=True)

    return kern


def stat_kernel(heads, c, sides, counted=False):
    def kern(*refs):
        q_refs, refs = refs[: len(sides)], refs[len(sides) :]
        st_in, refs = refs[0], refs[1:]
        if counted:
            cnt, refs = refs[0], refs[1:]
        k_ref, st_ref, e_ref = refs
        st_ref[...] = st_in[...]
        if counted:
            st_ref[37:38, :] = jnp.concatenate([cnt[0:1, :]] * (st_ref.shape[1] // 128), axis=1)
        for a, (q_ref, (base, begun)) in enumerate(zip(q_refs, sides)):
            for h in range(heads):
                scores = dg(k_ref[...], head(q_ref, h), 1, 1) * c
                top = jnp.max(scores, axis=0, keepdims=True)
                if begun:
                    m_old = st_ref[base + h : base + h + 1, :]
                    top = jnp.maximum(top, m_old)
                e = jnp.exp2(scores - top)
                total = jnp.sum(e, axis=0, keepdims=True)
                if begun:
                    total = total + st_ref[base + 8 + h : base + 9 + h, :] * jnp.exp2(m_old - top)
                e_ref[a * heads + h] = e.astype(bf16)
                st_ref[base + h : base + h + 1, :] = top
                st_ref[base + 8 + h : base + 9 + h, :] = total

    return kern


def join_kernel(offset):
    def kern(dn, own, up, *rest):
        near, pair = rest[-2:]
        n, width = own.shape
        for i, ref in enumerate((dn, own, up)):
            part = ref[...] if i == 1 else ref[:, offset : offset + width]
            near[i * n : (i + 1) * n, :] = part
            if i < 2:
                pair[i * n : (i + 1) * n, :] = part

    return kern


def merged_lse(m_one, l_one, m_two, l_two):
    top = jnp.maximum(m_one, m_two)
    return top + jnp.log2(l_one * jnp.exp2(m_one - top) + l_two * jnp.exp2(m_two - top))


def lse_of(st, rc, a, h):
    b = 16 - 16 * a
    o = 16 * a
    return merged_lse(
        st[o + h : o + h + 1, :],
        st[o + 8 + h : o + 9 + h, :],
        rc[b + h : b + h + 1, :],
        rc[b + 8 + h : b + 9 + h, :],
    )


def grad_kernel(heads, n_keys, split, n_tokens, has_in, last):
    def kern(qo, qp, go, gp, st, rc, mo, mp, k_ref, v_ref, *refs):
        e_refs, refs = refs[: 1 + split], refs[1 + split + n_tokens :]
        if has_in:
            dq_in, refs = refs[0], refs[1:]
        if last:
            kv_out, dq_out, dqp_out, dk_s, dv_s = refs
        else:
            kv_out, dq_out, dk_s, dv_s = refs
        k = k_ref[...]
        v = v_ref[...]
        kt = jnp.transpose(k)
        for a in range(2):
            for h in range(heads):
                q = head((qo, qp)[a], h)
                g = head((go, gp)[a], h)
                lse = lse_of(st, rc, a, h)
                delta = (st, rc)[a][32 + h : 33 + h, :]
                ratio = jnp.exp2((mo, mp)[a][16 * a + h : 16 * a + h + 1, :] - lse)
                e = e_refs[a][h] if split else e_refs[0][a * heads + h]
                p = e.astype(f32) * ratio
                ds = (p * (dg(v, g, 1, 1) - delta)).astype(bf16)
                dv = dg(p.astype(bf16), g, 1, 0)
                dk = dg(ds, q, 1, 0)
                if a == 0 and h == 0:
                    dk_s[...] = dk
                    dv_s[...] = dv
                else:
                    dk_s[...] += dk
                    dv_s[...] += dv
                i = a * heads + h
                dq = dg(kt, ds, 1, 0)
                if has_in:
                    dq = dq + dq_in[i]
                if last and a == 1:
                    dqp_out[h] = dq.astype(bf16)
                else:
                    dq_out[i] = dq
        count = st[37:38, :] + rc[37:38, :]
        step = n_keys + EXTRA
        for b in range(k.shape[0] // n_keys):
            part = pl.ds(b * n_keys, n_keys)
            kv_out[b * step : b * step + n_keys, :128] = dk_s[part, :].astype(kv_out.dtype)
            kv_out[b * step : b * step + n_keys, 128:] = dv_s[part, :].astype(kv_out.dtype)
            kv_out[b * step + n_keys : (b + 1) * step, :] = jnp.broadcast_to(
                count, (EXTRA, kv_out.shape[1])
            ).astype(kv_out.dtype)

    return kern


def comp_kernel(heads, c):
    def kern(q_ref, g_ref, st, rc, kc_ref, vc_ref, dq_in, kv_out, dq_out):
        mask = causal(st[38:39, :], q_ref.shape[0])
        k = kc_ref[...]
        v = vc_ref[...]
        kt = jnp.transpose(k)
        dk_sum = dv_sum = None
        for h in range(heads):
            q = head(q_ref, h)
            g = head(g_ref, h)
            lse = lse_of(st, rc, 0, h)
            delta = st[32 + h : 33 + h, :]
            s = jnp.where(mask, dg(k, q, 1, 1) * c, masked_score)
            p = jnp.exp2(s - lse)
            ds = (p * (dg(v, g, 1, 1) - delta)).astype(bf16)
            dv = dg(p.astype(bf16), g, 1, 0)
            dk = dg(ds, q, 1, 0)
            dk_sum = dk if h == 0 else dk_sum + dk
            dv_sum = dv if h == 0 else dv_sum + dv
            dq_out[h] = dq_in[h] + dg(kt, ds, 1, 0)
        kv_out[:, :128] = dk_sum
        kv_out[:, 128:] = dv_sum

    return kern


def up_kernel(n):
    def kern(own, three, up):
        up[...] = (own[2 * n :] + three[2 * n :].astype(f32)).astype(bf16)

    return kern


def down_kernel(n):
    def kern(own, three, two, unused, down, keep):
        down[...] = (own[:n] + three[:n].astype(f32) + two[:n].astype(f32)).astype(bf16)
        keep[...] = own[n : 2 * n] + three[n : 2 * n].astype(f32) + two[n:].astype(f32)

    return kern


def end_kernel(heads, scale, n_keys, all_slots):
    def kern(keep, one, two, ckv, dq_own, dq_rc, dq, dkc, dvc, dkp, dvp):
        kv = keep[...] + one[...].astype(f32) + two[...].astype(f32)
        factor = (all_slots / (BLOCK * kv[n_keys : n_keys + 1, :]))[:, :128]
        both = factor * scale
        dkp[...] = (kv[:n_keys, :128] * both).astype(bf16)
        dvp[...] = (kv[:n_keys, 128:] * factor).astype(bf16)
        dkc[...] = (ckv[:, :128] * both).astype(bf16)
        dvc[...] = (ckv[:, 128:] * factor).astype(bf16)
        for h in range(heads):
            t = jnp.transpose(dq_own[h] + dq_rc[h].astype(f32))
            dq[:, h * 128 : (h + 1) * 128] = (t * both).astype(bf16)

    return kern


def along_z(value, step, n_dp, n_z):
    pairs = []
    for d in range(n_dp):
        turn = step if d % 2 == 0 else -step
        for x in range(2):
            for z in range(n_z):
                source = (d * 2 + x) * n_z + z
                pairs.append((source, (d * 2 + x) * n_z + (z + turn) % n_z))
    return lax.ppermute(value, ("dp", "ctx"), pairs)


def across_x(value, n_z):
    return lax.ppermute(value, "ctx", [(i, (i + n_z) % (2 * n_z)) for i in range(2 * n_z)])


def per_device(
    q_comp, k_comp, v_comp, o_comp, d_out, k_prompt, v_prompt, kept_counts, comp_len, owner_list
):
    n_ctx = lax.axis_size("ctx")
    n_dp = lax.axis_size("dp")
    n_z = n_ctx // 2
    position = lax.axis_index("ctx")
    q, kc, vc = q_comp[0], k_comp[0], v_comp[0]
    o, d, k, v = o_comp[0], d_out[0], k_prompt[0], v_prompt[0]
    rows, width = q.shape
    n_keys, d_head = k.shape
    heads = width // d_head
    scale = d_head ** (-0.5)
    c = scale * LOG2E
    pair_flops = 2 * rows * heads * d_head

    lists = [kept_counts, comp_len, owner_list]

    def zmove(value, step):
        return along_z(value, step, n_dp, n_z)

    def after(value, *others):
        return lax.optimization_barrier((value, *others))[0]

    numbers = jnp.arange(comp_len.shape[1], dtype=jnp.int32)
    used = jnp.where(numbers < kept_counts[0], comp_len[0], 0)
    cnt = lax.ppermute(
        jnp.full((8, 128), jnp.sum(used).astype(f32)),
        ("dp", "ctx"),
        [(e * n_ctx + x, (e - x) % n_dp * n_ctx + x) for e in range(n_dp) for x in range(n_ctx)],
    )
    kv = call(
        pack_kernel,
        [sds((n_keys, 2 * d_head), bf16)],
        [k, v],
        hbm=(0, 1),
        scratch=[pltpu.SemaphoreType.DMA((2,))],
        vmem=62,
    )[0]
    kv_dn = zmove(kv, 3)
    kv_up = zmove(kv, -3)
    qp = across_x(q, n_z)
    st = call(
        first_kernel(heads, c),
        [sds((40, rows))],
        [*lists, q, kc, d, o],
        flops=pair_flops * (n_keys + rows) * 2,
        hbm=range(7),
        vmem=62,
        scratch=[pltpu.SMEM(x.shape, jnp.int32) for x in lists]
        + [pltpu.VMEM(x.shape, bf16) for x in (q, kc, d, o)]
        + [pltpu.SemaphoreType.DMA((7,))],
    )[0]

    def joined(own, offset, *tokens):
        return call(
            join_kernel(offset),
            [sds((3 * n_keys, d_head), bf16), sds((2 * n_keys, d_head), bf16)],
            [kv_dn, own, kv_up, *tokens],
        )

    def stats(q_list, st, k_set, sides, cnt=None):
        return call(
            stat_kernel(heads, c, sides, cnt is not None),
            [sds((40, rows)), sds((heads * len(q_list), k_set.shape[0], rows), bf16)],
            [*q_list, st] + ([] if cnt is None else [cnt]) + [k_set],
            flops=pair_flops * k_set.shape[0] * len(q_list) * 2,
        )

    own, partner = (0, True), (16, True)
    k_near, k_pair = joined(k, 0, st, cnt)
    k_three = zmove(k_near, 1)
    k_two = zmove(k_pair, -1)
    st_own, e_own = stats([q], st, k_near, [own], cnt)
    gp = across_x(after(d, qp, st_own), n_z)
    st_near, e_par = stats([qp], st_own, k_near, [(16, False)])
    v_near, v_pair = joined(v, d_head, st_near)
    v_three = zmove(v_near, 1)
    v_two = zmove(v_pair, -1)
    st_two, e_two = stats([q, qp], st_near, k_two, [own, partner])
    st, e_three = stats([q, qp], st_two, k_three, [own, partner])
    rc = across_x(st, n_z)

    def grads(k_set, v_set, m_own, m_par, e_sets, dq_in, out_type, tokens=()):
        total = k_set.shape[0]
        last = len(e_sets) == 2
        long = total // n_keys * (n_keys + EXTRA)
        outs = [sds((long, 2 * d_head), out_type)]
        outs.append(sds((heads if last else 2 * heads, d_head, rows)))
        if last:
            outs.append(sds((heads, d_head, rows), bf16))
        ins = [q, qp, d, gp, st, rc, m_own, m_par, k_set, v_set, *e_sets, *tokens]
        if dq_in is not None:
            ins.append(dq_in)
        return call(
            grad_kernel(heads, n_keys, last, len(tokens), dq_in is not None, last),
            outs,
            ins,
            scratch=[pltpu.VMEM((total, d_head), f32)] * 2,
        )

    kv_three, dq = grads(k_three, v_three, st, st, [e_three], None, bf16, [v_two])
    in_three = zmove(kv_three, -1)
    kv_two, dq = grads(k_two, v_two, st_two, st_two, [e_two], dq, bf16)
    in_two = zmove(kv_two, 1)
    kv_own, dq, dqp = grads(k_near, v_near, st_own, st_near, [e_own, e_par], dq, f32)
    block = (n_keys + EXTRA, 2 * d_head)
    up = call(up_kernel(block[0]), [sds(block, bf16)], [kv_own, in_three])[0]
    from_dn = zmove(up, 3)
    down, keep = call(
        down_kernel(block[0]), [sds(block, bf16), sds(block)], [kv_own, in_three, in_two, up]
    )
    from_up = zmove(down, -3)
    dq_rc = across_x(dqp, n_z)
    ckv, dq = call(
        comp_kernel(heads, c),
        [sds((rows, 2 * d_head)), sds((heads, d_head, rows))],
        [q, d, st, rc, kc, vc, dq],
        flops=pair_flops * rows * 5 * 2,
    )
    outs = call(
        end_kernel(heads, scale, n_keys, float(n_dp * n_ctx * rows)),
        [
            sds((rows, width), bf16),
            sds((rows, d_head), bf16),
            sds((rows, d_head), bf16),
            sds((n_keys, d_head), bf16),
            sds((n_keys, d_head), bf16),
        ],
        [keep, from_up, from_dn, ckv, dq, dq_rc],
    )
    return tuple(x[None] for x in outs)


def solution(mesh):
    split = P("dp", "ctx", None)
    return jax.shard_map(
        per_device,
        mesh=mesh,
        in_specs=(split,) * 7 + (P("dp"), P("dp", None), P("dp", None)),
        out_specs=(split,) * 5,
        check_vma=False,
    )
```

```python
import jax
import jax.numpy as jnp
from jax import lax
from jax.experimental import pallas as pl
from jax.experimental.pallas import tpu as pltpu
from jax.sharding import PartitionSpec as P

BLOCK = 128
EXTRA = 16
LOG2E = 1.4426950408889634
masked_score = -1e30
f32 = jnp.float32
bf16 = jnp.bfloat16


def dg(a, b, ca, cb):
    return lax.dot_general(a, b, (((ca,), (cb,)), ((), ())), preferred_element_type=f32)


def call(kern, outs, ins, flops=0, hbm=(), anywhere=(), scratch=(), vmem=24):
    total = sum(x.size * x.dtype.itemsize for x in ins) + sum(
        o.size * o.dtype.itemsize for o in outs
    )
    spaces = {**{i: pltpu.HBM for i in hbm}, **{i: pl.ANY for i in anywhere}}
    specs = [pl.BlockSpec(memory_space=spaces.get(i, pltpu.VMEM)) for i in range(len(ins))]
    ins = [
        pltpu.with_memory_space_constraint(x, pltpu.HBM) if i in hbm else x
        for i, x in enumerate(ins)
    ]
    return pl.pallas_call(
        kern,
        out_shape=outs,
        in_specs=specs,
        out_specs=[pl.BlockSpec(memory_space=pltpu.VMEM)] * len(outs),
        scratch_shapes=list(scratch),
        compiler_params=pltpu.CompilerParams(vmem_limit_bytes=vmem * 2**20),
        cost_estimate=pl.CostEstimate(flops=int(flops), bytes_accessed=1, transcendentals=0),
    )(*ins)


def sds(shape, dtype=f32):
    return jax.ShapeDtypeStruct(shape, dtype)


def head(ref, h):
    return ref[:, h * 128 : (h + 1) * 128]


def run_info(kept, lens, owners, position):
    blocks = same = jnp.int32(0)
    for j in range(lens.shape[1]):
        n = jnp.where(j < kept[0], lens[0, j], 0)
        mine = jnp.where(owners[0, j] == position, n, 0)
        blocks = blocks + mine
        same = jnp.maximum(same, mine - 1)
    return blocks, same


def causal(same, n):
    key = lax.broadcasted_iota(jnp.int32, (n, n), 0)
    row = lax.broadcasted_iota(jnp.int32, (n, n), 1)
    same_block = (key // BLOCK) == (row // BLOCK)
    return (key <= row) & (same_block | (same > 0))


def pack_kernel(k_any, v_any, kv_ref, sems):
    width = k_any.shape[1]
    one = pltpu.make_async_copy(k_any, kv_ref.at[:, :width], sems.at[0])
    two = pltpu.make_async_copy(v_any, kv_ref.at[:, width:], sems.at[1])
    one.start()
    two.start()
    one.wait()
    two.wait()


def first_kernel(heads, c):
    def kern(
        kept_any, lens_any, owners_any, q_any, kc_any, d_any, o_any, vc_any,
        st_ref, q_ref, kc_ref, d_ref, vc_ref,
        kept, lens, owners, o_ref, sems,
    ):
        pairs = (
            (kept_any, kept), (lens_any, lens), (owners_any, owners),
            (q_any, q_ref), (kc_any, kc_ref), (d_any, d_ref), (o_any, o_ref),
            (vc_any, vc_ref),
        )
        copies = [pltpu.make_async_copy(x, y, sems.at[i]) for i, (x, y) in enumerate(pairs)]
        for copy in copies:
            copy.start()
        for copy in copies[:3]:
            copy.wait()
        rows = q_ref.shape[0]
        blocks, same = run_info(kept, lens, owners, lax.axis_index("ctx"))
        empty = lax.broadcasted_iota(jnp.int32, (1, rows), 1) // BLOCK >= blocks
        mask = causal(same, rows)
        st_ref[...] = jnp.zeros_like(st_ref)
        st_ref[38:39, :] = jnp.full((1, rows), same.astype(f32))
        for copy in copies[3:5]:
            copy.wait()
        kc = kc_ref[...]
        for h in range(heads):
            q = head(q_ref, h)
            comp = jnp.where(mask, dg(kc, q, 1, 1) * c, masked_score)
            top = jnp.max(comp, axis=0, keepdims=True)
            total = jnp.sum(jnp.exp2(comp - top), axis=0, keepdims=True)
            st_ref[h : h + 1, :] = jnp.where(empty, -masked_score, top)
            st_ref[8 + h : 9 + h, :] = jnp.where(empty, 1.0, total)
        for copy in copies[5:]:
            copy.wait()
        for h in range(heads):
            prod = head(d_ref, h).astype(f32) * head(o_ref, h).astype(f32)
            st_ref[32 + h : 33 + h, :] = jnp.sum(jnp.transpose(prod), axis=0, keepdims=True)

    return kern


def stat_kernel(heads, c, sides, counted=False):
    def kern(*refs):
        q_refs, refs = refs[: len(sides)], refs[len(sides) :]
        st_in, refs = refs[0], refs[1:]
        if counted:
            cnt, refs = refs[0], refs[1:]
        k_ref, st_ref, e_ref = refs
        st_ref[...] = st_in[...]
        if counted:
            st_ref[37:38, :] = jnp.concatenate([cnt[0:1, :]] * (st_ref.shape[1] // 128), axis=1)
        for a, (q_ref, (base, begun)) in enumerate(zip(q_refs, sides)):
            for h in range(heads):
                scores = dg(k_ref[...], head(q_ref, h), 1, 1) * c
                top = jnp.max(scores, axis=0, keepdims=True)
                if begun:
                    m_old = st_ref[base + h : base + h + 1, :]
                    top = jnp.maximum(top, m_old)
                e = jnp.exp2(scores - top)
                total = jnp.sum(e, axis=0, keepdims=True)
                if begun:
                    total = total + st_ref[base + 8 + h : base + 9 + h, :] * jnp.exp2(m_old - top)
                e_ref[a * heads + h] = e.astype(bf16)
                st_ref[base + h : base + h + 1, :] = top
                st_ref[base + 8 + h : base + 9 + h, :] = total

    return kern


def join_kernel(offset, width):
    def kern(dn, own, up, *rest):
        near, pair = rest[-2:]
        n = own.shape[0]
        for i, ref in enumerate((dn, own, up)):
            part = ref[:, offset : offset + width]
            near[i * n : (i + 1) * n, :] = part
            if i < 2:
                pair[i * n : (i + 1) * n, :] = part

    return kern


def merged_lse(m_one, l_one, m_two, l_two):
    top = jnp.maximum(m_one, m_two)
    return top + jnp.log2(l_one * jnp.exp2(m_one - top) + l_two * jnp.exp2(m_two - top))


def lse_of(st, rc, a, h):
    b = 16 - 16 * a
    o = 16 * a
    return merged_lse(
        st[o + h : o + h + 1, :],
        st[o + 8 + h : o + 9 + h, :],
        rc[b + h : b + h + 1, :],
        rc[b + 8 + h : b + 9 + h, :],
    )


def grad_kernel(heads, n_keys, split, n_tokens, has_in, last):
    def kern(qo, qp, go, gp, st, rc, mo, mp, k_ref, v_ref, *refs):
        e_refs, refs = refs[: 1 + split], refs[1 + split + n_tokens :]
        if has_in:
            dq_in, refs = refs[0], refs[1:]
        if last:
            kv_out, dq_out, dqp_out, dk_s, dv_s = refs
        else:
            kv_out, dq_out, dk_s, dv_s = refs
        k = k_ref[...]
        v = v_ref[...]
        kt = jnp.transpose(k)
        for a in range(2):
            for h in range(heads):
                q = head((qo, qp)[a], h)
                g = head((go, gp)[a], h)
                lse = lse_of(st, rc, a, h)
                delta = (st, rc)[a][32 + h : 33 + h, :]
                ratio = jnp.exp2((mo, mp)[a][16 * a + h : 16 * a + h + 1, :] - lse)
                e = e_refs[a][h] if split else e_refs[0][a * heads + h]
                p = e.astype(f32) * ratio
                ds = (p * (dg(v, g, 1, 1) - delta)).astype(bf16)
                dv = dg(p.astype(bf16), g, 1, 0)
                dk = dg(ds, q, 1, 0)
                if a == 0 and h == 0:
                    dk_s[...] = dk
                    dv_s[...] = dv
                else:
                    dk_s[...] += dk
                    dv_s[...] += dv
                i = a * heads + h
                dq = dg(kt, ds, 1, 0)
                if has_in:
                    dq = dq + dq_in[i]
                if last and a == 1:
                    dqp_out[h] = dq.astype(bf16)
                else:
                    dq_out[i] = dq
        count = st[37:38, :] + rc[37:38, :]
        step = n_keys + EXTRA
        for b in range(k.shape[0] // n_keys):
            part = pl.ds(b * n_keys, n_keys)
            kv_out[b * step : b * step + n_keys, :128] = dk_s[part, :].astype(kv_out.dtype)
            kv_out[b * step : b * step + n_keys, 128:] = dv_s[part, :].astype(kv_out.dtype)
            kv_out[b * step + n_keys : (b + 1) * step, :] = jnp.broadcast_to(
                count, (EXTRA, kv_out.shape[1])
            ).astype(kv_out.dtype)

    return kern


def comp_kernel(heads, c):
    def kern(q_ref, g_ref, st, rc, kc_ref, vc_ref, dq_in, kv_out, dq_out):
        mask = causal(st[38:39, :], q_ref.shape[0])
        k = kc_ref[...]
        v = vc_ref[...]
        kt = jnp.transpose(k)
        dk_sum = dv_sum = None
        for h in range(heads):
            q = head(q_ref, h)
            g = head(g_ref, h)
            lse = lse_of(st, rc, 0, h)
            delta = st[32 + h : 33 + h, :]
            s = jnp.where(mask, dg(k, q, 1, 1) * c, masked_score)
            p = jnp.exp2(s - lse)
            ds = (p * (dg(v, g, 1, 1) - delta)).astype(bf16)
            dv = dg(p.astype(bf16), g, 1, 0)
            dk = dg(ds, q, 1, 0)
            dk_sum = dk if h == 0 else dk_sum + dk
            dv_sum = dv if h == 0 else dv_sum + dv
            dq_out[h] = dq_in[h] + dg(kt, ds, 1, 0)
        kv_out[:, :128] = dk_sum
        kv_out[:, 128:] = dv_sum

    return kern


def up_kernel(n):
    def kern(own, three, up):
        up[...] = (own[2 * n :] + three[2 * n :].astype(f32)).astype(bf16)

    return kern


def down_kernel(n):
    def kern(own, three, two, unused, down, keep):
        down[...] = (own[:n] + three[:n].astype(f32) + two[:n].astype(f32)).astype(bf16)
        keep[...] = own[n : 2 * n] + three[n : 2 * n].astype(f32) + two[n:].astype(f32)

    return kern


def end_kernel(heads, scale, n_keys, all_slots):
    def kern(keep, one, two, ckv, dq_own, dq_rc, dq, dkc, dvc, dkp, dvp):
        kv = keep[...] + one[...].astype(f32) + two[...].astype(f32)
        factor = (all_slots / (BLOCK * kv[n_keys : n_keys + 1, :]))[:, :128]
        both = factor * scale
        dkp[...] = (kv[:n_keys, :128] * both).astype(bf16)
        dvp[...] = (kv[:n_keys, 128:] * factor).astype(bf16)
        dkc[...] = (ckv[:, :128] * both).astype(bf16)
        dvc[...] = (ckv[:, 128:] * factor).astype(bf16)
        for h in range(heads):
            t = jnp.transpose(dq_own[h] + dq_rc[h].astype(f32))
            dq[:, h * 128 : (h + 1) * 128] = (t * both).astype(bf16)

    return kern


def along_z(value, step, n_dp, n_z):
    pairs = []
    for d in range(n_dp):
        turn = step if d % 2 == 0 else -step
        for x in range(2):
            for z in range(n_z):
                source = (d * 2 + x) * n_z + z
                pairs.append((source, (d * 2 + x) * n_z + (z + turn) % n_z))
    return lax.ppermute(value, ("dp", "ctx"), pairs)


def across_x(value, n_z):
    return lax.ppermute(value, "ctx", [(i, (i + n_z) % (2 * n_z)) for i in range(2 * n_z)])


def per_device(
    q_comp, k_comp, v_comp, o_comp, d_out, k_prompt, v_prompt, kept_counts, comp_len, owner_list
):
    n_ctx = lax.axis_size("ctx")
    n_dp = lax.axis_size("dp")
    n_z = n_ctx // 2
    position = lax.axis_index("ctx")
    q, kc, vc = q_comp[0], k_comp[0], v_comp[0]
    o, d, k, v = o_comp[0], d_out[0], k_prompt[0], v_prompt[0]
    rows, width = q.shape
    n_keys, d_head = k.shape
    heads = width // d_head
    scale = d_head ** (-0.5)
    c = scale * LOG2E
    pair_flops = 2 * rows * heads * d_head

    lists = [kept_counts, comp_len, owner_list]

    def zmove(value, step):
        return along_z(value, step, n_dp, n_z)

    def after(value, *others):
        return lax.optimization_barrier((value, *others))[0]

    numbers = jnp.arange(comp_len.shape[1], dtype=jnp.int32)
    used = jnp.where(numbers < kept_counts[0], comp_len[0], 0)
    cnt = lax.ppermute(
        jnp.full((8, 128), jnp.sum(used).astype(f32)),
        ("dp", "ctx"),
        [(e * n_ctx + x, (e - x) % n_dp * n_ctx + x) for e in range(n_dp) for x in range(n_ctx)],
    )
    kv = call(
        pack_kernel,
        [sds((n_keys, 2 * d_head), bf16)],
        [k, v],
        hbm=(0, 1),
        scratch=[pltpu.SemaphoreType.DMA((2,))],
    )[0]
    kv_dn = zmove(kv, 3)
    kv_up = zmove(kv, -3)
    qp = across_x(q, n_z)
    st, q, kc, d, vc = call(
        first_kernel(heads, c),
        [sds((40, rows))] + [sds(x.shape, bf16) for x in (q, kc, d, vc)],
        [*lists, q, kc, d, o, vc],
        flops=pair_flops * (n_keys + rows) * 2,
        hbm=range(1, 8),
        anywhere=(0,),
        scratch=[pltpu.SMEM(x.shape, jnp.int32) for x in lists]
        + [pltpu.VMEM(o.shape, bf16), pltpu.SemaphoreType.DMA((8,))],
    )

    def joined(offset, *tokens):
        return call(
            join_kernel(offset, d_head),
            [sds((3 * n_keys, d_head), bf16), sds((2 * n_keys, d_head), bf16)],
            [kv_dn, kv, kv_up, *tokens],
        )

    def stats(q_list, st, k_set, sides, cnt=None):
        return call(
            stat_kernel(heads, c, sides, cnt is not None),
            [sds((40, rows)), sds((heads * len(q_list), k_set.shape[0], rows), bf16)],
            [*q_list, st] + ([] if cnt is None else [cnt]) + [k_set],
            flops=pair_flops * k_set.shape[0] * len(q_list) * 2,
        )

    own, partner = (0, True), (16, True)
    k_near, k_pair = joined(0, st, cnt)
    k_three = zmove(k_near, 1)
    k_two = zmove(k_pair, -1)
    st_own, e_own = stats([q], st, k_near, [own], cnt)
    gp = across_x(after(d, qp, st_own), n_z)
    st_near, e_par = stats([qp], st_own, k_near, [(16, False)])
    v_near, v_pair = joined(d_head, st_near)
    v_three = zmove(v_near, 1)
    v_two = zmove(v_pair, -1)
    st_two, e_two = stats([q, qp], st_near, k_two, [own, partner])
    st, e_three = stats([q, qp], st_two, k_three, [own, partner])
    rc = across_x(st, n_z)

    def grads(k_set, v_set, m_own, m_par, e_sets, dq_in, out_type, tokens=()):
        total = k_set.shape[0]
        last = len(e_sets) == 2
        long = total // n_keys * (n_keys + EXTRA)
        outs = [sds((long, 2 * d_head), out_type)]
        outs.append(sds((heads if last else 2 * heads, d_head, rows)))
        if last:
            outs.append(sds((heads, d_head, rows), bf16))
        ins = [q, qp, d, gp, st, rc, m_own, m_par, k_set, v_set, *e_sets, *tokens]
        if dq_in is not None:
            ins.append(dq_in)
        return call(
            grad_kernel(heads, n_keys, last, len(tokens), dq_in is not None, last),
            outs,
            ins,
            scratch=[pltpu.VMEM((total, d_head), f32)] * 2,
        )

    kv_three, dq = grads(k_three, v_three, st, st, [e_three], None, bf16, [v_two])
    in_three = zmove(kv_three, -1)
    kv_two, dq = grads(k_two, v_two, st_two, st_two, [e_two], dq, bf16)
    in_two = zmove(kv_two, 1)
    kv_own, dq, dqp = grads(k_near, v_near, st_own, st_near, [e_own, e_par], dq, f32)
    block = (n_keys + EXTRA, 2 * d_head)
    up = call(up_kernel(block[0]), [sds(block, bf16)], [kv_own, in_three])[0]
    from_dn = zmove(up, 3)
    down, keep = call(
        down_kernel(block[0]), [sds(block, bf16), sds(block)], [kv_own, in_three, in_two, up]
    )
    from_up = zmove(down, -3)
    dq_rc = across_x(dqp, n_z)
    ckv, dq = call(
        comp_kernel(heads, c),
        [sds((rows, 2 * d_head)), sds((heads, d_head, rows))],
        [q, d, st, rc, kc, vc, dq],
        flops=pair_flops * rows * 5 * 2,
    )
    outs = call(
        end_kernel(heads, scale, n_keys, float(n_dp * n_ctx * rows)),
        [
            sds((rows, width), bf16),
            sds((rows, d_head), bf16),
            sds((rows, d_head), bf16),
            sds((n_keys, d_head), bf16),
            sds((n_keys, d_head), bf16),
        ],
        [keep, from_up, from_dn, ckv, dq, dq_rc],
    )
    return tuple(x[None] for x in outs)


def solution(mesh):
    split = P("dp", "ctx", None)
    return jax.shard_map(
        per_device,
        mesh=mesh,
        in_specs=(split,) * 7 + (P("dp"), P("dp", None), P("dp", None)),
        out_specs=(split,) * 5,
        check_vma=False,
    )
```

```python
import jax
import jax.numpy as jnp
from jax import lax
from jax.experimental import pallas as pl
from jax.experimental.pallas import tpu as pltpu
from jax.sharding import PartitionSpec as P

BLOCK = 128
EXTRA = 16
LOG2E = 1.4426950408889634
masked_score = -1e30
f32 = jnp.float32
bf16 = jnp.bfloat16


def dg(a, b, ca, cb):
    return lax.dot_general(a, b, (((ca,), (cb,)), ((), ())), preferred_element_type=f32)


def call(kern, outs, ins, flops=0, hbm=(), anywhere=(), scratch=(), vmem=16):
    total = sum(x.size * x.dtype.itemsize for x in ins) + sum(
        o.size * o.dtype.itemsize for o in outs
    )
    spaces = {**{i: pltpu.HBM for i in hbm}, **{i: pl.ANY for i in anywhere}}
    specs = [pl.BlockSpec(memory_space=spaces.get(i, pltpu.VMEM)) for i in range(len(ins))]
    ins = [
        pltpu.with_memory_space_constraint(x, pltpu.HBM) if i in hbm else x
        for i, x in enumerate(ins)
    ]
    return pl.pallas_call(
        kern,
        out_shape=outs,
        in_specs=specs,
        out_specs=[pl.BlockSpec(memory_space=pltpu.VMEM)] * len(outs),
        scratch_shapes=list(scratch),
        compiler_params=pltpu.CompilerParams(vmem_limit_bytes=vmem * 2**20),
        cost_estimate=pl.CostEstimate(flops=int(flops), bytes_accessed=1, transcendentals=0),
    )(*ins)


def sds(shape, dtype=f32):
    return jax.ShapeDtypeStruct(shape, dtype)


def head(ref, h, rows=None):
    return ref[:rows, h * 128 : (h + 1) * 128]


def delta_of(ref, rows, h):
    parts = ref[rows : rows + EXTRA, :rows].astype(f32)
    return parts[3 * h : 3 * h + 1] + parts[3 * h + 1 : 3 * h + 2] + parts[3 * h + 2 : 3 * h + 3]


def run_info(kept, lens, owners, position):
    blocks = same = jnp.int32(0)
    for j in range(lens.shape[1]):
        n = jnp.where(j < kept[0], lens[0, j], 0)
        mine = jnp.where(owners[0, j] == position, n, 0)
        blocks = blocks + mine
        same = jnp.maximum(same, mine - 1)
    return blocks, same


def causal(same, n):
    key = lax.broadcasted_iota(jnp.int32, (n, n), 0)
    row = lax.broadcasted_iota(jnp.int32, (n, n), 1)
    same_block = (key // BLOCK) == (row // BLOCK)
    return (key <= row) & (same_block | (same > 0))


def pack_kernel(k_any, v_any, kv_ref, sems):
    width = k_any.shape[1]
    one = pltpu.make_async_copy(k_any, kv_ref.at[:, :width], sems.at[0])
    two = pltpu.make_async_copy(v_any, kv_ref.at[:, width:], sems.at[1])
    one.start()
    two.start()
    one.wait()
    two.wait()


def first_kernel(heads, c):
    def kern(
        kept_any, lens_any, owners_any, q_any, kc_any, d_any, o_any, vc_any,
        st_ref, q_ref, kc_ref, d_ref, vc_ref,
        kept, lens, owners, o_ref, sems,
    ):
        pairs = (
            (kept_any, kept), (lens_any, lens), (owners_any, owners),
            (q_any, q_ref), (kc_any, kc_ref), (d_any, d_ref.at[pl.ds(0, q_any.shape[0]), :]),
            (o_any, o_ref),
            (vc_any, vc_ref),
        )
        copies = [pltpu.make_async_copy(x, y, sems.at[i]) for i, (x, y) in enumerate(pairs)]
        for copy in copies:
            copy.start()
        for copy in copies[:3]:
            copy.wait()
        rows = q_ref.shape[0]
        blocks, same = run_info(kept, lens, owners, lax.axis_index("ctx"))
        empty = lax.broadcasted_iota(jnp.int32, (1, rows), 1) // BLOCK >= blocks
        mask = causal(same, rows)
        st_ref[...] = jnp.zeros_like(st_ref)
        st_ref[38:39, :] = jnp.full((1, rows), same.astype(f32))
        for copy in copies[3:5]:
            copy.wait()
        kc = kc_ref[...]
        for h in range(heads):
            q = head(q_ref, h)
            comp = jnp.where(mask, dg(kc, q, 1, 1) * c, masked_score)
            top = jnp.max(comp, axis=0, keepdims=True)
            total = jnp.sum(jnp.exp2(comp - top), axis=0, keepdims=True)
            st_ref[h : h + 1, :] = jnp.where(empty, -masked_score, top)
            st_ref[8 + h : 9 + h, :] = jnp.where(empty, 1.0, total)
        for copy in copies[5:]:
            copy.wait()
        parts = []
        for h in range(heads):
            prod = head(d_ref, h, rows).astype(f32) * head(o_ref, h).astype(f32)
            delta = jnp.sum(jnp.transpose(prod), axis=0, keepdims=True)
            st_ref[32 + h : 33 + h, :] = delta
            high = delta.astype(bf16).astype(f32)
            mid = (delta - high).astype(bf16).astype(f32)
            parts += [high, mid, delta - high - mid]
        parts.append(jnp.zeros((EXTRA - len(parts), rows), f32))
        d_ref[rows : rows + EXTRA, :] = jnp.zeros((EXTRA, d_ref.shape[1]), bf16)
        d_ref[rows : rows + EXTRA, :rows] = jnp.concatenate(parts, axis=0).astype(bf16)

    return kern


def stat_kernel(heads, c, sides, counted=False):
    def kern(*refs):
        q_refs, refs = refs[: len(sides)], refs[len(sides) :]
        st_in, refs = refs[0], refs[1:]
        if counted:
            cnt, refs = refs[0], refs[1:]
        k_ref, st_ref, e_ref = refs
        st_ref[...] = st_in[...]
        if counted:
            st_ref[37:38, :] = jnp.concatenate([cnt[0:1, :]] * (st_ref.shape[1] // 128), axis=1)
        for a, (q_ref, (base, begun)) in enumerate(zip(q_refs, sides)):
            for h in range(heads):
                scores = dg(k_ref[...], head(q_ref, h), 1, 1) * c
                top = jnp.max(scores, axis=0, keepdims=True)
                if begun:
                    m_old = st_ref[base + h : base + h + 1, :]
                    top = jnp.maximum(top, m_old)
                e = jnp.exp2(scores - top)
                total = jnp.sum(e, axis=0, keepdims=True)
                if begun:
                    total = total + st_ref[base + 8 + h : base + 9 + h, :] * jnp.exp2(m_old - top)
                e_ref[a * heads + h] = e.astype(bf16)
                st_ref[base + h : base + h + 1, :] = top
                st_ref[base + 8 + h : base + 9 + h, :] = total

    return kern


def join_kernel(offset, width):
    def kern(dn, own, up, *rest):
        near, pair = rest[-2:]
        n = own.shape[0]
        for i, ref in enumerate((dn, own, up)):
            part = ref[:, offset : offset + width]
            near[i * n : (i + 1) * n, :] = part
            if i < 2:
                pair[i * n : (i + 1) * n, :] = part

    return kern


def merged_lse(m_one, l_one, m_two, l_two):
    top = jnp.maximum(m_one, m_two)
    return top + jnp.log2(l_one * jnp.exp2(m_one - top) + l_two * jnp.exp2(m_two - top))


def lse_of(st, rc, a, h):
    b = 16 - 16 * a
    o = 16 * a
    return merged_lse(
        st[o + h : o + h + 1, :],
        st[o + 8 + h : o + 9 + h, :],
        rc[b + h : b + h + 1, :],
        rc[b + 8 + h : b + 9 + h, :],
    )


def early_kernel(heads, split, n_tokens):
    def kern(go, gp, k_ref, v_ref, *refs):
        e_refs, (ds_out, dq_out) = refs[: 1 + split], refs[1 + split + n_tokens :]
        rows = e_refs[0].shape[2]
        v = v_ref[...]
        kt = jnp.transpose(k_ref[...])
        for a in range(2):
            for h in range(heads):
                i = a * heads + h
                g = head((go, gp)[a], h, rows)
                delta = delta_of((go, gp)[a], rows, h)
                e = e_refs[a][h] if split else e_refs[0][i]
                ds_out[i] = (e.astype(f32) * (dg(v, g, 1, 1) - delta)).astype(bf16)
        for i in range(2 * heads):
            dq_out[i] = dg(kt, ds_out[i], 1, 0)

    return kern


def ratio_of(st, rc, top, a, h):
    i = 16 * a + h
    return jnp.exp2(top[i : i + 1, :] - lse_of(st, rc, a, h))


def late_kernel(heads, n_keys, split, n_tokens):
    def kern(qo, qp, go, gp, st, rc, mo, mp, ds_ref, *refs):
        e_refs, (kv_out, dk_s, dv_s, q_s, g_s) = refs[: 1 + split], refs[1 + split + n_tokens :]
        rows = qo.shape[0]
        for a in range(2):
            for h in range(heads):
                i = a * heads + h
                ratio = ratio_of(st, rc, (mo, mp)[a], a, h)
                column = jnp.transpose(jnp.broadcast_to(ratio, (128, rows)))
                q_s[i] = (head((qo, qp)[a], h).astype(f32) * column).astype(bf16)
                g_s[i] = (head((go, gp)[a], h, rows).astype(f32) * column).astype(bf16)
        for a in range(2):
            for h in range(heads):
                i = a * heads + h
                e = e_refs[a][h] if split else e_refs[0][i]
                dv = dg(e, g_s[i], 1, 0)
                dk = dg(ds_ref[i], q_s[i], 1, 0)
                if i == 0:
                    dk_s[...] = dk
                    dv_s[...] = dv
                else:
                    dk_s[...] += dk
                    dv_s[...] += dv
        count = st[37:38, :] + rc[37:38, :]
        step = n_keys + EXTRA
        for b in range(ds_ref.shape[1] // n_keys):
            part = pl.ds(b * n_keys, n_keys)
            kv_out[b * step : b * step + n_keys, :128] = dk_s[part, :].astype(kv_out.dtype)
            kv_out[b * step : b * step + n_keys, 128:] = dv_s[part, :].astype(kv_out.dtype)
            kv_out[b * step + n_keys : (b + 1) * step, :] = jnp.broadcast_to(
                count, (EXTRA, kv_out.shape[1])
            ).astype(kv_out.dtype)

    return kern


def query_kernel(heads):
    def kern(st, rc, st_own, st_near, st_two, near, two, three, unused, own_out, partner_out):
        for a in range(2):
            for h in range(heads):
                i = a * heads + h
                total = near[i] * ratio_of(st, rc, (st_own, st_near)[a], a, h)
                total = total + two[i] * ratio_of(st, rc, st_two, a, h)
                total = total + three[i] * ratio_of(st, rc, st, a, h)
                if a == 0:
                    own_out[h] = total
                else:
                    partner_out[h] = total.astype(bf16)

    return kern


def comp_kernel(heads, c):
    def kern(q_ref, g_ref, st, rc, kc_ref, vc_ref, dq_in, kv_out, dq_out):
        mask = causal(st[38:39, :], q_ref.shape[0])
        k = kc_ref[...]
        v = vc_ref[...]
        kt = jnp.transpose(k)
        dk_sum = dv_sum = None
        for h in range(heads):
            q = head(q_ref, h)
            g = head(g_ref, h, q_ref.shape[0])
            lse = lse_of(st, rc, 0, h)
            delta = st[32 + h : 33 + h, :]
            s = jnp.where(mask, dg(k, q, 1, 1) * c, masked_score)
            p = jnp.exp2(s - lse)
            ds = (p * (dg(v, g, 1, 1) - delta)).astype(bf16)
            dv = dg(p.astype(bf16), g, 1, 0)
            dk = dg(ds, q, 1, 0)
            dk_sum = dk if h == 0 else dk_sum + dk
            dv_sum = dv if h == 0 else dv_sum + dv
            dq_out[h] = dq_in[h] + dg(kt, ds, 1, 0)
        kv_out[:, :128] = dk_sum
        kv_out[:, 128:] = dv_sum

    return kern


def up_kernel(n):
    def kern(near, three, up):
        up[...] = (near[2 * n :] + three[2 * n :].astype(f32)).astype(bf16)

    return kern


def down_kernel(n):
    def kern(near, three, two, unused, down, keep):
        down[...] = (near[:n] + three[:n].astype(f32) + two[:n].astype(f32)).astype(bf16)
        keep[...] = near[n : 2 * n] + three[n : 2 * n].astype(f32) + two[n:].astype(f32)

    return kern


def turn_kernel(heads):
    def kern(dq_own, dq_rc, out):
        for h in range(heads):
            out[:, h * 128 : (h + 1) * 128] = jnp.transpose(dq_own[h] + dq_rc[h].astype(f32))

    return kern


def end_kernel(scale, n_keys, all_slots):
    def kern(keep, one_rc, two_rc, ckv, dq_sum, dq, dkc, dvc, dkp, dvp):
        kv = keep[...] + one_rc[...].astype(f32) + two_rc[...].astype(f32)
        factor = (all_slots / (BLOCK * kv[n_keys : n_keys + 1, :]))[:, :128]
        both = factor * scale
        dkp[...] = (kv[:n_keys, :128] * both).astype(bf16)
        dvp[...] = (kv[:n_keys, 128:] * factor).astype(bf16)
        dkc[...] = (ckv[:, :128] * both).astype(bf16)
        dvc[...] = (ckv[:, 128:] * factor).astype(bf16)
        for h in range(dq.shape[1] // 128):
            dq[:, h * 128 : (h + 1) * 128] = (head(dq_sum, h) * both).astype(bf16)

    return kern


def along_z(value, step, n_dp, n_z):
    pairs = []
    for d in range(n_dp):
        turn = step if d % 2 == 0 else -step
        for x in range(2):
            for z in range(n_z):
                source = (d * 2 + x) * n_z + z
                pairs.append((source, (d * 2 + x) * n_z + (z + turn) % n_z))
    return lax.ppermute(value, ("dp", "ctx"), pairs)


def across_x(value, n_z):
    return lax.ppermute(value, "ctx", [(i, (i + n_z) % (2 * n_z)) for i in range(2 * n_z)])


def per_device(
    q_comp, k_comp, v_comp, o_comp, d_out, k_prompt, v_prompt, kept_counts, comp_len, owner_list
):
    n_ctx = lax.axis_size("ctx")
    n_dp = lax.axis_size("dp")
    n_z = n_ctx // 2
    position = lax.axis_index("ctx")
    q, kc, vc = q_comp[0], k_comp[0], v_comp[0]
    o, d, k, v = o_comp[0], d_out[0], k_prompt[0], v_prompt[0]
    rows, width = q.shape
    n_keys, d_head = k.shape
    heads = width // d_head
    scale = d_head ** (-0.5)
    c = scale * LOG2E
    pair_flops = 2 * rows * heads * d_head

    lists = [kept_counts, comp_len, owner_list]

    def zmove(value, step):
        return along_z(value, step, n_dp, n_z)

    def after(value, *others):
        return lax.optimization_barrier((value, *others))[0]

    numbers = jnp.arange(comp_len.shape[1], dtype=jnp.int32)
    used = jnp.where(numbers < kept_counts[0], comp_len[0], 0)
    cnt = lax.ppermute(
        jnp.full((8, 128), jnp.sum(used).astype(f32)),
        ("dp", "ctx"),
        [(e * n_ctx + x, (e - x) % n_dp * n_ctx + x) for e in range(n_dp) for x in range(n_ctx)],
    )
    kv = call(
        pack_kernel,
        [sds((n_keys, 2 * d_head), bf16)],
        [k, v],
        hbm=(0, 1),
        scratch=[pltpu.SemaphoreType.DMA((2,))],
    )[0]
    kv_dn = zmove(kv, 3)
    kv_up = zmove(kv, -3)
    qp = across_x(q, n_z)
    st, q, kc, d, vc = call(
        first_kernel(heads, c),
        [sds((40, rows))]
        + [sds(x, bf16) for x in (q.shape, kc.shape, (rows + EXTRA, width), vc.shape)],
        [*lists, q, kc, d, o, vc],
        flops=pair_flops * (n_keys + rows) * 2,
        hbm=range(1, 8),
        anywhere=(0,),
        scratch=[pltpu.SMEM(x.shape, jnp.int32) for x in lists]
        + [pltpu.VMEM(o.shape, bf16), pltpu.SemaphoreType.DMA((8,))],
    )

    def joined(offset, *tokens):
        return call(
            join_kernel(offset, d_head),
            [sds((3 * n_keys, d_head), bf16), sds((2 * n_keys, d_head), bf16)],
            [kv_dn, kv, kv_up, *tokens],
        )

    def stats(q_list, st, k_set, sides, cnt=None):
        return call(
            stat_kernel(heads, c, sides, cnt is not None),
            [sds((40, rows)), sds((heads * len(q_list), k_set.shape[0], rows), bf16)],
            [*q_list, st] + ([] if cnt is None else [cnt]) + [k_set],
            flops=pair_flops * k_set.shape[0] * len(q_list) * 2,
        )

    own, partner = (0, True), (16, True)
    k_near, k_pair = joined(0, st, cnt)
    k_three = zmove(k_near, 1)
    k_two = zmove(k_pair, -1)
    st_own, e_own = stats([q], st, k_near, [own], cnt)
    gp = across_x(after(d, qp, st_own), n_z)
    st_near, e_par = stats([qp], st_own, k_near, [(16, False)])
    v_near, v_pair = joined(d_head, st_near)
    v_three = zmove(v_near, 1)
    v_two = zmove(v_pair, -1)
    st_two, e_two = stats([q, qp], st_near, k_two, [own, partner])
    st, e_three = stats([q, qp], st_two, k_three, [own, partner])
    rc = across_x(st, n_z)

    def early(k_set, v_set, e_sets, token):
        return call(
            early_kernel(heads, len(e_sets) == 2, 1),
            [sds((2 * heads, k_set.shape[0], rows), bf16), sds((2 * heads, d_head, rows))],
            [d, gp, k_set, v_set, *e_sets, token],
        )

    def late(ds, m_own, m_par, e_sets, out_type, token):
        total = ds.shape[1]
        return call(
            late_kernel(heads, n_keys, len(e_sets) == 2, 1),
            [sds((total // n_keys * (n_keys + EXTRA), 2 * d_head), out_type)],
            [q, qp, d, gp, st, rc, m_own, m_par, ds, *e_sets, token],
            scratch=[pltpu.VMEM((total, d_head), f32)] * 2
            + [pltpu.VMEM((2 * heads, rows, d_head), bf16)] * 2,
        )[0]

    ds_three, dq_three = early(k_three, v_three, [e_three], st)
    kv_three = late(ds_three, st, st, [e_three], bf16, v_two)
    in_three = zmove(kv_three, -1)
    ds_two, dq_two = early(k_two, v_two, [e_two], kv_three)
    kv_two = late(ds_two, st_two, st_two, [e_two], bf16, dq_two)
    in_two = zmove(kv_two, 1)
    ds_near, dq_near = early(k_near, v_near, [e_own, e_par], kv_two)
    kv_near = late(ds_near, st_own, st_near, [e_own, e_par], f32, dq_near)
    dq, dqp = call(
        query_kernel(heads),
        [sds((heads, d_head, rows)), sds((heads, d_head, rows), bf16)],
        [st, rc, st_own, st_near, st_two, dq_near, dq_two, dq_three, kv_near],
    )
    block = (n_keys + EXTRA, 2 * d_head)
    up = call(up_kernel(block[0]), [sds(block, bf16)], [kv_near, in_three])[0]
    from_dn = zmove(up, 3)
    dq_rc = across_x(dqp, n_z)
    down, keep = call(
        down_kernel(block[0]),
        [sds(block, bf16), sds(block)],
        [kv_near, in_three, in_two, up],
    )
    from_up = zmove(down, -3)
    ckv, dq = call(
        comp_kernel(heads, c),
        [sds((rows, 2 * d_head)), sds((heads, d_head, rows))],
        [q, d, st, rc, kc, vc, dq],
    )
    dq = call(turn_kernel(heads), [sds((rows, width))], [dq, dq_rc])[0]
    outs = call(
        end_kernel(scale, n_keys, float(n_dp * n_ctx * rows)),
        [
            sds((rows, width), bf16),
            sds((rows, d_head), bf16),
            sds((rows, d_head), bf16),
            sds((n_keys, d_head), bf16),
            sds((n_keys, d_head), bf16),
        ],
        [keep, from_up, from_dn, ckv, dq],
    )
    return tuple(x[None] for x in outs)


def solution(mesh):
    split = P("dp", "ctx", None)
    return jax.shard_map(
        per_device,
        mesh=mesh,
        in_specs=(split,) * 7 + (P("dp"), P("dp", None), P("dp", None)),
        out_specs=(split,) * 5,
        check_vma=False,
    )
```

```python
import jax
import jax.numpy as jnp
from jax import lax
from jax.experimental import pallas as pl
from jax.experimental.pallas import tpu as pltpu
from jax.sharding import PartitionSpec as P

BLOCK = 128
EXTRA = 16
FAR = 40.0
LOG2E = 1.4426950408889634
masked_score = -1e30
f32 = jnp.float32
bf16 = jnp.bfloat16


def dg(a, b, ca, cb):
    return lax.dot_general(a, b, (((ca,), (cb,)), ((), ())), preferred_element_type=f32)


def call(kern, outs, ins, flops=0, hbm=(), anywhere=(), scratch=(), vmem=16):
    total = sum(x.size * x.dtype.itemsize for x in ins) + sum(
        o.size * o.dtype.itemsize for o in outs
    )
    spaces = {**{i: pltpu.HBM for i in hbm}, **{i: pl.ANY for i in anywhere}}
    specs = [pl.BlockSpec(memory_space=spaces.get(i, pltpu.VMEM)) for i in range(len(ins))]
    ins = [
        pltpu.with_memory_space_constraint(x, pltpu.HBM) if i in hbm else x
        for i, x in enumerate(ins)
    ]
    return pl.pallas_call(
        kern,
        out_shape=outs,
        in_specs=specs,
        out_specs=[pl.BlockSpec(memory_space=pltpu.VMEM)] * len(outs),
        scratch_shapes=list(scratch),
        compiler_params=pltpu.CompilerParams(vmem_limit_bytes=vmem * 2**20),
        cost_estimate=pl.CostEstimate(flops=int(flops), bytes_accessed=1, transcendentals=0),
    )(*ins)


def sds(shape, dtype=f32):
    return jax.ShapeDtypeStruct(shape, dtype)


def head(ref, h, rows=None):
    return ref[:rows, h * 128 : (h + 1) * 128]


def delta_of(ref, rows, h):
    parts = ref[rows : rows + EXTRA, :rows].astype(f32)
    return parts[3 * h : 3 * h + 1] + parts[3 * h + 1 : 3 * h + 2] + parts[3 * h + 2 : 3 * h + 3]


def run_info(kept, lens, owners, position):
    blocks = same = used = jnp.int32(0)
    for j in range(lens.shape[1]):
        n = jnp.where(j < kept[0], lens[0, j], 0)
        mine = jnp.where(owners[0, j] == position, n, 0)
        used = used + n
        blocks = blocks + mine
        same = jnp.maximum(same, mine - 1)
    return blocks, same, used


def causal(same, n):
    key = lax.broadcasted_iota(jnp.int32, (n, n), 0)
    row = lax.broadcasted_iota(jnp.int32, (n, n), 1)
    same_block = (key // BLOCK) == (row // BLOCK)
    return (key <= row) & (same_block | (same > 0))


def pack_kernel(k_any, v_any, kv_ref, sems):
    width = k_any.shape[1]
    one = pltpu.make_async_copy(k_any, kv_ref.at[:, :width], sems.at[0])
    two = pltpu.make_async_copy(v_any, kv_ref.at[:, width:], sems.at[1])
    one.start()
    two.start()
    one.wait()
    two.wait()


def first_kernel(heads, c):
    def kern(
        kept_any, lens_any, owners_any, q_any, kc_any, d_any, o_any, vc_any,
        st_ref, cnt_ref, q_ref, kc_ref, d_ref, vc_ref,
        kept, lens, owners, o_ref, sems,
    ):
        pairs = (
            (kept_any, kept), (lens_any, lens), (owners_any, owners),
            (q_any, q_ref), (kc_any, kc_ref), (d_any, d_ref.at[pl.ds(0, q_any.shape[0]), :]),
            (o_any, o_ref),
            (vc_any, vc_ref),
        )
        copies = [pltpu.make_async_copy(x, y, sems.at[i]) for i, (x, y) in enumerate(pairs)]
        for copy in copies:
            copy.start()
        for copy in copies[:3]:
            copy.wait()
        rows = q_ref.shape[0]
        blocks, same, used = run_info(kept, lens, owners, lax.axis_index("ctx"))
        empty = lax.broadcasted_iota(jnp.int32, (1, rows), 1) // BLOCK >= blocks
        mask = causal(same, rows)
        st_ref[...] = jnp.zeros_like(st_ref)
        cnt_ref[...] = jnp.full(cnt_ref.shape, used.astype(f32))
        st_ref[38:39, :] = jnp.full((1, rows), same.astype(f32))
        for copy in copies[3:5]:
            copy.wait()
        kc = kc_ref[...]
        for h in range(heads):
            q = head(q_ref, h)
            comp = jnp.where(mask, dg(kc, q, 1, 1) * c, masked_score)
            top = jnp.max(comp, axis=0, keepdims=True)
            total = jnp.sum(jnp.exp2(comp - top), axis=0, keepdims=True)
            st_ref[h : h + 1, :] = jnp.where(empty, -masked_score, top)
            st_ref[8 + h : 9 + h, :] = jnp.where(empty, 1.0, total)
        for copy in copies[5:]:
            copy.wait()
        parts = []
        for h in range(heads):
            prod = head(d_ref, h, rows).astype(f32) * head(o_ref, h).astype(f32)
            delta = jnp.sum(jnp.transpose(prod), axis=0, keepdims=True)
            st_ref[32 + h : 33 + h, :] = delta
            high = delta.astype(bf16).astype(f32)
            mid = (delta - high).astype(bf16).astype(f32)
            parts += [high, mid, delta - high - mid]
        parts.append(jnp.zeros((EXTRA - len(parts), rows), f32))
        d_ref[rows : rows + EXTRA, :] = jnp.zeros((EXTRA, d_ref.shape[1]), bf16)
        d_ref[rows : rows + EXTRA, :rows] = jnp.concatenate(parts, axis=0).astype(bf16)

    return kern


def stat_kernel(heads, c, sides, counted=False):
    def kern(*refs):
        q_refs, refs = refs[: len(sides)], refs[len(sides) :]
        st_in, refs = refs[0], refs[1:]
        if counted:
            cnt, refs = refs[0], refs[1:]
        k_ref, st_ref, e_ref = refs
        st_ref[...] = st_in[...]
        if counted:
            st_ref[37:38, :] = jnp.concatenate([cnt[0:1, :]] * (st_ref.shape[1] // 128), axis=1)

        def score(a, h):
            return dg(k_ref[...], head(q_refs[a], h), 1, 1) * c

        def rows_of(a, h):
            base = sides[a][0]
            return slice(base + h, base + h + 1), slice(base + 8 + h, base + 9 + h)

        def exact(a, h, source):
            m_row, l_row = rows_of(a, h)
            scores = score(a, h)
            top = jnp.max(scores, axis=0, keepdims=True)
            if sides[a][1]:
                m_old = source[m_row, :]
                top = jnp.maximum(top, m_old)
            e = jnp.exp2(scores - top)
            total = jnp.sum(e, axis=0, keepdims=True)
            if sides[a][1]:
                total = total + source[l_row, :] * jnp.exp2(m_old - top)
            e_ref[a * heads + h] = e.astype(bf16)
            st_ref[m_row, :] = top
            st_ref[l_row, :] = total

        begun = [a for a in range(len(sides)) if sides[a][1]]
        for a in range(len(sides)):
            for h in range(heads if a not in begun else 0):
                exact(a, h, st_in)
        worst = None
        for a in begun:
            for h in range(heads):
                m_row, l_row = rows_of(a, h)
                above = score(a, h) - st_in[m_row, :]
                e = jnp.exp2(above)
                e_ref[a * heads + h] = e.astype(bf16)
                st_ref[l_row, :] = st_in[l_row, :] + jnp.sum(e, axis=0, keepdims=True)
                high = jnp.max(above, axis=0, keepdims=True)
                worst = high if worst is None else jnp.maximum(worst, high)
        if begun:

            @pl.when(jnp.max(worst) > FAR)
            def _():
                for a in begun:
                    for h in range(heads):
                        exact(a, h, st_in)

    return kern


def join_kernel(offset, width):
    def kern(dn, own, up, *rest):
        near, pair = rest[-2:]
        n = own.shape[0]
        for i, ref in enumerate((dn, own, up)):
            part = ref[:, offset : offset + width]
            near[i * n : (i + 1) * n, :] = part
            if i < 2:
                pair[i * n : (i + 1) * n, :] = part

    return kern


def merged_lse(m_one, l_one, m_two, l_two):
    top = jnp.maximum(m_one, m_two)
    return top + jnp.log2(l_one * jnp.exp2(m_one - top) + l_two * jnp.exp2(m_two - top))


def lse_of(st, rc, a, h):
    b = 16 - 16 * a
    o = 16 * a
    return merged_lse(
        st[o + h : o + h + 1, :],
        st[o + 8 + h : o + 9 + h, :],
        rc[b + h : b + h + 1, :],
        rc[b + 8 + h : b + 9 + h, :],
    )


def early_kernel(heads, split, n_tokens):
    def kern(go, gp, k_ref, v_ref, *refs):
        e_refs, (ds_out, dq_out) = refs[: 1 + split], refs[1 + split + n_tokens :]
        rows = e_refs[0].shape[2]
        v = v_ref[...]
        kt = jnp.transpose(k_ref[...])
        for a in range(2):
            for h in range(heads):
                i = a * heads + h
                g = head((go, gp)[a], h, rows)
                delta = delta_of((go, gp)[a], rows, h)
                e = e_refs[a][h] if split else e_refs[0][i]
                ds_out[i] = (e.astype(f32) * (dg(v, g, 1, 1) - delta)).astype(bf16)
        for i in range(2 * heads):
            dq_out[i] = dg(kt, ds_out[i], 1, 0)

    return kern


def ratio_of(st, rc, top, a, h):
    i = 16 * a + h
    return jnp.exp2(top[i : i + 1, :] - lse_of(st, rc, a, h))


def late_kernel(heads, n_keys, split, n_tokens):
    def kern(qo, qp, go, gp, st, rc, mo, mp, ds_ref, *refs):
        e_refs, (kv_out, dk_s, dv_s, q_s, g_s) = refs[: 1 + split], refs[1 + split + n_tokens :]
        rows = qo.shape[0]
        for a in range(2):
            for h in range(heads):
                i = a * heads + h
                ratio = ratio_of(st, rc, (mo, mp)[a], a, h)
                column = jnp.transpose(jnp.broadcast_to(ratio, (128, rows)))
                q_s[i] = (head((qo, qp)[a], h).astype(f32) * column).astype(bf16)
                g_s[i] = (head((go, gp)[a], h, rows).astype(f32) * column).astype(bf16)
        for a in range(2):
            for h in range(heads):
                i = a * heads + h
                e = e_refs[a][h] if split else e_refs[0][i]
                dv = dg(e, g_s[i], 1, 0)
                dk = dg(ds_ref[i], q_s[i], 1, 0)
                if i == 0:
                    dk_s[...] = dk
                    dv_s[...] = dv
                else:
                    dk_s[...] += dk
                    dv_s[...] += dv
        count = st[37:38, :] + rc[37:38, :]
        step = n_keys + EXTRA
        for b in range(ds_ref.shape[1] // n_keys):
            part = pl.ds(b * n_keys, n_keys)
            kv_out[b * step : b * step + n_keys, :128] = dk_s[part, :].astype(kv_out.dtype)
            kv_out[b * step : b * step + n_keys, 128:] = dv_s[part, :].astype(kv_out.dtype)
            kv_out[b * step + n_keys : (b + 1) * step, :] = jnp.broadcast_to(
                count, (EXTRA, kv_out.shape[1])
            ).astype(kv_out.dtype)

    return kern


def query_kernel(heads):
    def kern(st, rc, st_own, st_near, st_two, near, two, three, unused, own_out, partner_out):
        for a in range(2):
            for h in range(heads):
                i = a * heads + h
                total = near[i] * ratio_of(st, rc, (st_own, st_near)[a], a, h)
                total = total + two[i] * ratio_of(st, rc, st_two, a, h)
                total = total + three[i] * ratio_of(st, rc, st, a, h)
                if a == 0:
                    own_out[h] = total
                else:
                    partner_out[h] = total.astype(bf16)

    return kern


def comp_kernel(heads, c):
    def kern(q_ref, g_ref, st, rc, kc_ref, vc_ref, dq_in, kv_out, dq_out):
        mask = causal(st[38:39, :], q_ref.shape[0])
        k = kc_ref[...]
        v = vc_ref[...]
        kt = jnp.transpose(k)
        dk_sum = dv_sum = None
        for h in range(heads):
            q = head(q_ref, h)
            g = head(g_ref, h, q_ref.shape[0])
            lse = lse_of(st, rc, 0, h)
            delta = st[32 + h : 33 + h, :]
            s = jnp.where(mask, dg(k, q, 1, 1) * c, masked_score)
            p = jnp.exp2(s - lse)
            ds = (p * (dg(v, g, 1, 1) - delta)).astype(bf16)
            dv = dg(p.astype(bf16), g, 1, 0)
            dk = dg(ds, q, 1, 0)
            dk_sum = dk if h == 0 else dk_sum + dk
            dv_sum = dv if h == 0 else dv_sum + dv
            dq_out[h] = dq_in[h] + dg(kt, ds, 1, 0)
        kv_out[:, :128] = dk_sum
        kv_out[:, 128:] = dv_sum

    return kern


def up_kernel(n):
    def kern(near, three, up):
        up[...] = (near[2 * n :] + three[2 * n :].astype(f32)).astype(bf16)

    return kern


def down_kernel(n):
    def kern(near, three, two, unused, down, keep):
        down[...] = (near[:n] + three[:n].astype(f32) + two[:n].astype(f32)).astype(bf16)
        keep[...] = near[n : 2 * n] + three[n : 2 * n].astype(f32) + two[n:].astype(f32)

    return kern


def turn_kernel(heads):
    def kern(dq_own, dq_rc, unused, out):
        for h in range(heads):
            out[:, h * 128 : (h + 1) * 128] = jnp.transpose(dq_own[h] + dq_rc[h].astype(f32))

    return kern


def end_kernel(scale, n_keys, all_slots):
    def kern(keep, one_rc, two_rc, ckv, dq_sum, dq, dkc, dvc, dkp, dvp):
        kv = keep[...] + one_rc[...].astype(f32) + two_rc[...].astype(f32)
        factor = (all_slots / (BLOCK * kv[n_keys : n_keys + 1, :]))[:, :128]
        both = factor * scale
        dkp[...] = (kv[:n_keys, :128] * both).astype(bf16)
        dvp[...] = (kv[:n_keys, 128:] * factor).astype(bf16)
        dkc[...] = (ckv[:, :128] * both).astype(bf16)
        dvc[...] = (ckv[:, 128:] * factor).astype(bf16)
        for h in range(dq.shape[1] // 128):
            dq[:, h * 128 : (h + 1) * 128] = (head(dq_sum, h) * both).astype(bf16)

    return kern


def along_z(value, step, n_dp, n_z):
    pairs = []
    for d in range(n_dp):
        turn = step if d % 2 == 0 else -step
        for x in range(2):
            for z in range(n_z):
                source = (d * 2 + x) * n_z + z
                pairs.append((source, (d * 2 + x) * n_z + (z + turn) % n_z))
    return lax.ppermute(value, ("dp", "ctx"), pairs)


def across_x(value, n_z):
    return lax.ppermute(value, "ctx", [(i, (i + n_z) % (2 * n_z)) for i in range(2 * n_z)])


def per_device(
    q_comp, k_comp, v_comp, o_comp, d_out, k_prompt, v_prompt, kept_counts, comp_len, owner_list
):
    n_ctx = lax.axis_size("ctx")
    n_dp = lax.axis_size("dp")
    n_z = n_ctx // 2
    position = lax.axis_index("ctx")
    q, kc, vc = q_comp[0], k_comp[0], v_comp[0]
    o, d, k, v = o_comp[0], d_out[0], k_prompt[0], v_prompt[0]
    rows, width = q.shape
    n_keys, d_head = k.shape
    heads = width // d_head
    scale = d_head ** (-0.5)
    c = scale * LOG2E
    pair_flops = 2 * rows * heads * d_head

    lists = [kept_counts, comp_len, owner_list]

    def zmove(value, step):
        return along_z(value, step, n_dp, n_z)

    def after(value, *others):
        return lax.optimization_barrier((value, *others))[0]

    kv = call(
        pack_kernel,
        [sds((n_keys, 2 * d_head), bf16)],
        [k, v],
        hbm=(0, 1),
        scratch=[pltpu.SemaphoreType.DMA((2,))],
    )[0]
    kv_dn = zmove(kv, 3)
    kv_up = zmove(kv, -3)
    qp = across_x(q, n_z)
    st, cnt, q, kc, d, vc = call(
        first_kernel(heads, c),
        [sds((40, rows)), sds((8, 128))]
        + [sds(x, bf16) for x in (q.shape, kc.shape, (rows + EXTRA, width), vc.shape)],
        [*lists, q, kc, d, o, vc],
        flops=pair_flops * (n_keys + rows) * 2,
        hbm=range(1, 8),
        anywhere=(0,),
        scratch=[pltpu.SMEM(x.shape, jnp.int32) for x in lists]
        + [pltpu.VMEM(o.shape, bf16), pltpu.SemaphoreType.DMA((8,))],
    )

    cnt = lax.ppermute(
        cnt,
        ("dp", "ctx"),
        [(e * n_ctx + x, (e - x) % n_dp * n_ctx + x) for e in range(n_dp) for x in range(n_ctx)],
    )

    def joined(offset, *tokens):
        return call(
            join_kernel(offset, d_head),
            [sds((3 * n_keys, d_head), bf16), sds((2 * n_keys, d_head), bf16)],
            [kv_dn, kv, kv_up, *tokens],
        )

    def stats(q_list, st, k_set, sides, cnt=None):
        return call(
            stat_kernel(heads, c, sides, cnt is not None),
            [sds((40, rows)), sds((heads * len(q_list), k_set.shape[0], rows), bf16)],
            [*q_list, st] + ([] if cnt is None else [cnt]) + [k_set],
            flops=pair_flops * k_set.shape[0] * len(q_list) * 2,
        )

    own, partner = (0, True), (16, True)
    k_near, k_pair = joined(0, st, cnt)
    k_three = zmove(k_near, 1)
    k_two = zmove(k_pair, -1)
    st_own, e_own = stats([q], st, k_near, [own], cnt)
    gp = across_x(after(d, qp, st_own), n_z)
    st_near, e_par = stats([qp], st_own, k_near, [(16, False)])
    v_near, v_pair = joined(d_head, st_near)
    v_three = zmove(v_near, 1)
    v_two = zmove(v_pair, -1)
    st_two, e_two = stats([q, qp], st_near, k_two, [own, partner])
    st, e_three = stats([q, qp], st_two, k_three, [own, partner])
    rc = across_x(st, n_z)

    def early(k_set, v_set, e_sets, token):
        return call(
            early_kernel(heads, len(e_sets) == 2, 1),
            [sds((2 * heads, k_set.shape[0], rows), bf16), sds((2 * heads, d_head, rows))],
            [d, gp, k_set, v_set, *e_sets, token],
        )

    def late(ds, m_own, m_par, e_sets, out_type, token):
        total = ds.shape[1]
        return call(
            late_kernel(heads, n_keys, len(e_sets) == 2, 1),
            [sds((total // n_keys * (n_keys + EXTRA), 2 * d_head), out_type)],
            [q, qp, d, gp, st, rc, m_own, m_par, ds, *e_sets, token],
            scratch=[pltpu.VMEM((total, d_head), f32)] * 2
            + [pltpu.VMEM((2 * heads, rows, d_head), bf16)] * 2,
        )[0]

    ds_three, dq_three = early(k_three, v_three, [e_three], st)
    kv_three = late(ds_three, st, st, [e_three], bf16, v_two)
    in_three = zmove(kv_three, -1)
    ds_two, dq_two = early(k_two, v_two, [e_two], kv_three)
    kv_two = late(ds_two, st_two, st_two, [e_two], bf16, dq_two)
    in_two = zmove(kv_two, 1)
    ds_near, dq_near = early(k_near, v_near, [e_own, e_par], kv_two)
    dq, dqp = call(
        query_kernel(heads),
        [sds((heads, d_head, rows)), sds((heads, d_head, rows), bf16)],
        [st, rc, st_own, st_near, st_two, dq_near, dq_two, dq_three, kv_two],
    )
    dq_rc = across_x(dqp, n_z)
    kv_near = late(ds_near, st_own, st_near, [e_own, e_par], f32, dqp)
    block = (n_keys + EXTRA, 2 * d_head)
    up = call(up_kernel(block[0]), [sds(block, bf16)], [kv_near, in_three])[0]
    from_dn = zmove(up, 3)
    down, keep = call(
        down_kernel(block[0]),
        [sds(block, bf16), sds(block)],
        [kv_near, in_three, in_two, up],
    )
    from_up = zmove(down, -3)
    ckv, dq = call(
        comp_kernel(heads, c),
        [sds((rows, 2 * d_head)), sds((heads, d_head, rows))],
        [q, d, st, rc, kc, vc, dq],
    )
    dq = call(turn_kernel(heads), [sds((rows, width))], [dq, dq_rc, from_dn])[0]
    outs = call(
        end_kernel(scale, n_keys, float(n_dp * n_ctx * rows)),
        [
            sds((rows, width), bf16),
            sds((rows, d_head), bf16),
            sds((rows, d_head), bf16),
            sds((n_keys, d_head), bf16),
            sds((n_keys, d_head), bf16),
        ],
        [keep, from_dn, from_up, ckv, dq],
    )
    return tuple(x[None] for x in outs)


def solution(mesh):
    split = P("dp", "ctx", None)
    return jax.shard_map(
        per_device,
        mesh=mesh,
        in_specs=(split,) * 7 + (P("dp"), P("dp", None), P("dp", None)),
        out_specs=(split,) * 5,
        check_vma=False,
    )
```

```python
import jax
import jax.numpy as jnp
from jax import lax
from jax.experimental import pallas as pl
from jax.experimental.pallas import tpu as pltpu
from jax.sharding import PartitionSpec as P

BLOCK = 128
EXTRA = 16
FAR = 40.0
LOG2E = 1.4426950408889634
masked_score = -1e30
f32 = jnp.float32
bf16 = jnp.bfloat16


def dg(a, b, ca, cb):
    return lax.dot_general(a, b, (((ca,), (cb,)), ((), ())), preferred_element_type=f32)


def call(kern, outs, ins, flops=0, hbm=(), anywhere=(), scratch=(), vmem=16):
    total = sum(x.size * x.dtype.itemsize for x in ins) + sum(
        o.size * o.dtype.itemsize for o in outs
    )
    spaces = {**{i: pltpu.HBM for i in hbm}, **{i: pl.ANY for i in anywhere}}
    specs = [pl.BlockSpec(memory_space=spaces.get(i, pltpu.VMEM)) for i in range(len(ins))]
    ins = [
        pltpu.with_memory_space_constraint(x, pltpu.HBM) if i in hbm else x
        for i, x in enumerate(ins)
    ]
    return pl.pallas_call(
        kern,
        out_shape=outs,
        in_specs=specs,
        out_specs=[pl.BlockSpec(memory_space=pltpu.VMEM)] * len(outs),
        scratch_shapes=list(scratch),
        compiler_params=pltpu.CompilerParams(vmem_limit_bytes=vmem * 2**20),
        cost_estimate=pl.CostEstimate(flops=int(flops), bytes_accessed=1, transcendentals=0),
    )(*ins)


def sds(shape, dtype=f32):
    return jax.ShapeDtypeStruct(shape, dtype)


def head(ref, h, rows=None):
    if isinstance(h, int):
        return ref[:rows, h * 128 : (h + 1) * 128]
    return ref[:rows, pl.ds(pl.multiple_of(h * 128, 128), 128)]


def row(ref, i):
    return ref[pl.ds(i, 1), :]


def delta_of(ref, rows, h):
    parts = ref[rows : rows + EXTRA, :rows].astype(f32)
    return parts[3 * h : 3 * h + 1] + parts[3 * h + 1 : 3 * h + 2] + parts[3 * h + 2 : 3 * h + 3]


def run_info(kept, lens, owners, position):
    blocks = same = used = jnp.int32(0)
    for j in range(lens.shape[1]):
        n = jnp.where(j < kept[0], lens[0, j], 0)
        mine = jnp.where(owners[0, j] == position, n, 0)
        used = used + n
        blocks = blocks + mine
        same = jnp.maximum(same, mine - 1)
    return blocks, same, used


def causal(same, n):
    key = lax.broadcasted_iota(jnp.int32, (n, n), 0)
    row = lax.broadcasted_iota(jnp.int32, (n, n), 1)
    same_block = (key // BLOCK) == (row // BLOCK)
    return (key <= row) & (same_block | (same > 0))


def pack_kernel(k_any, v_any, kv_ref, sems):
    width = k_any.shape[1]
    one = pltpu.make_async_copy(k_any, kv_ref.at[:, :width], sems.at[0])
    two = pltpu.make_async_copy(v_any, kv_ref.at[:, width:], sems.at[1])
    one.start()
    two.start()
    one.wait()
    two.wait()


def first_kernel(heads, c):
    def kern(
        kept_any, lens_any, owners_any, q_any, kc_any, d_any, o_any, vc_any,
        st_ref, cnt_ref, q_ref, kc_ref, d_ref, vc_ref,
        kept, lens, owners, o_ref, sems,
    ):
        pairs = (
            (kept_any, kept), (lens_any, lens), (owners_any, owners),
            (q_any, q_ref), (kc_any, kc_ref), (d_any, d_ref.at[pl.ds(0, q_any.shape[0]), :]),
            (o_any, o_ref),
            (vc_any, vc_ref),
        )
        copies = [pltpu.make_async_copy(x, y, sems.at[i]) for i, (x, y) in enumerate(pairs)]
        for copy in copies:
            copy.start()
        for copy in copies[:3]:
            copy.wait()
        rows = q_ref.shape[0]
        blocks, same, used = run_info(kept, lens, owners, lax.axis_index("ctx"))
        empty = lax.broadcasted_iota(jnp.int32, (1, rows), 1) // BLOCK >= blocks
        mask = causal(same, rows)
        st_ref[...] = jnp.zeros_like(st_ref)
        cnt_ref[...] = jnp.full(cnt_ref.shape, used.astype(f32))
        st_ref[38:39, :] = jnp.full((1, rows), same.astype(f32))
        for copy in copies[3:5]:
            copy.wait()
        kc = kc_ref[...]
        for h in range(heads):
            q = head(q_ref, h)
            comp = jnp.where(mask, dg(kc, q, 1, 1) * c, masked_score)
            top = jnp.max(comp, axis=0, keepdims=True)
            total = jnp.sum(jnp.exp2(comp - top), axis=0, keepdims=True)
            st_ref[h : h + 1, :] = jnp.where(empty, -masked_score, top)
            st_ref[8 + h : 9 + h, :] = jnp.where(empty, 1.0, total)
        for copy in copies[5:]:
            copy.wait()
        parts = []
        for h in range(heads):
            prod = head(d_ref, h, rows).astype(f32) * head(o_ref, h).astype(f32)
            delta = jnp.sum(jnp.transpose(prod), axis=0, keepdims=True)
            st_ref[32 + h : 33 + h, :] = delta
            high = delta.astype(bf16).astype(f32)
            mid = (delta - high).astype(bf16).astype(f32)
            parts += [high, mid, delta - high - mid]
        parts.append(jnp.zeros((EXTRA - len(parts), rows), f32))
        d_ref[rows : rows + EXTRA, :] = jnp.zeros((EXTRA, d_ref.shape[1]), bf16)
        d_ref[rows : rows + EXTRA, :rows] = jnp.concatenate(parts, axis=0).astype(bf16)

    return kern


def stat_kernel(heads, c, sides, counted=False):
    def kern(*refs):
        q_refs, refs = refs[: len(sides)], refs[len(sides) :]
        st_in, refs = refs[0], refs[1:]
        if counted:
            cnt, refs = refs[0], refs[1:]
        k_ref, st_ref, e_ref = refs
        st_ref[...] = st_in[...]
        if counted:
            st_ref[37:38, :] = jnp.concatenate([cnt[0:1, :]] * (st_ref.shape[1] // 128), axis=1)

        def score(a, h):
            return dg(k_ref[...], head(q_refs[a], h), 1, 1) * c

        def rows_of(a, h):
            base = sides[a][0]
            return pl.ds(base + h, 1), pl.ds(base + 8 + h, 1)

        def exact(a, h, source):
            m_row, l_row = rows_of(a, h)
            scores = score(a, h)
            top = jnp.max(scores, axis=0, keepdims=True)
            if sides[a][1]:
                m_old = source[m_row, :]
                top = jnp.maximum(top, m_old)
            e = jnp.exp2(scores - top)
            total = jnp.sum(e, axis=0, keepdims=True)
            if sides[a][1]:
                total = total + source[l_row, :] * jnp.exp2(m_old - top)
            e_ref[a * heads + h] = e.astype(bf16)
            st_ref[m_row, :] = top
            st_ref[l_row, :] = total

        begun = [a for a in range(len(sides)) if sides[a][1]]
        for a in range(len(sides)):
            for h in range(heads if a not in begun else 0):
                exact(a, h, st_in)
        worst = None
        for a in begun:
            for h in range(heads):
                m_row, l_row = rows_of(a, h)
                above = score(a, h) - st_in[m_row, :]
                e = jnp.exp2(above)
                e_ref[a * heads + h] = e.astype(bf16)
                st_ref[l_row, :] = st_in[l_row, :] + jnp.sum(e, axis=0, keepdims=True)
                high = jnp.max(above, axis=0, keepdims=True)
                worst = high if worst is None else jnp.maximum(worst, high)
        if begun:

            @pl.when(jnp.max(worst) > FAR)
            def _():
                for a in begun:

                    @pl.loop(0, heads)
                    def _(h):
                        exact(a, h, st_in)

    return kern


def join_kernel(offset, width):
    def kern(dn, own, up, *rest):
        near, pair = rest[-2:]
        n = own.shape[0]
        for i, ref in enumerate((dn, own, up)):
            part = ref[:, offset : offset + width]
            near[i * n : (i + 1) * n, :] = part
            if i < 2:
                pair[i * n : (i + 1) * n, :] = part

    return kern


def merged_lse(m_one, l_one, m_two, l_two):
    top = jnp.maximum(m_one, m_two)
    return top + jnp.log2(l_one * jnp.exp2(m_one - top) + l_two * jnp.exp2(m_two - top))


def lse_of(st, rc, a, h):
    b = 16 - 16 * a
    o = 16 * a
    return merged_lse(row(st, o + h), row(st, o + 8 + h), row(rc, b + h), row(rc, b + 8 + h))


def early_kernel(heads, split, n_tokens):
    def kern(go, gp, k_ref, v_ref, *refs):
        e_refs, (ds_out, dq_out) = refs[: 1 + split], refs[1 + split + n_tokens :]
        rows = e_refs[0].shape[2]
        v = v_ref[...]
        kt = jnp.transpose(k_ref[...])
        for a in range(2):
            for h in range(heads):
                i = a * heads + h
                g = head((go, gp)[a], h, rows)
                delta = delta_of((go, gp)[a], rows, h)
                e = e_refs[a][h] if split else e_refs[0][i]
                ds_out[i] = (e.astype(f32) * (dg(v, g, 1, 1) - delta)).astype(bf16)
        for i in range(2 * heads):
            dq_out[i] = dg(kt, ds_out[i], 1, 0)

    return kern


def ratio_of(st, rc, top, a, h):
    i = 16 * a + h
    return jnp.exp2(top[i : i + 1, :] - lse_of(st, rc, a, h))


def late_kernel(heads, n_keys, split, n_tokens):
    def kern(qo, qp, go, gp, st, rc, mo, mp, ds_ref, *refs):
        e_refs, (kv_out, dk_s, dv_s, q_s, g_s) = refs[: 1 + split], refs[1 + split + n_tokens :]
        rows = qo.shape[0]
        for a in range(2):
            for h in range(heads):
                i = a * heads + h
                ratio = ratio_of(st, rc, (mo, mp)[a], a, h)
                column = jnp.transpose(jnp.broadcast_to(ratio, (128, rows)))
                q_s[i] = (head((qo, qp)[a], h).astype(f32) * column).astype(bf16)
                g_s[i] = (head((go, gp)[a], h, rows).astype(f32) * column).astype(bf16)
        for a in range(2):
            for h in range(heads):
                i = a * heads + h
                e = e_refs[a][h] if split else e_refs[0][i]
                dv = dg(e, g_s[i], 1, 0)
                dk = dg(ds_ref[i], q_s[i], 1, 0)
                if i == 0:
                    dk_s[...] = dk
                    dv_s[...] = dv
                else:
                    dk_s[...] += dk
                    dv_s[...] += dv
        count = st[37:38, :] + rc[37:38, :]
        step = n_keys + EXTRA
        for b in range(ds_ref.shape[1] // n_keys):
            part = pl.ds(b * n_keys, n_keys)
            kv_out[b * step : b * step + n_keys, :128] = dk_s[part, :].astype(kv_out.dtype)
            kv_out[b * step : b * step + n_keys, 128:] = dv_s[part, :].astype(kv_out.dtype)
            kv_out[b * step + n_keys : (b + 1) * step, :] = jnp.broadcast_to(
                count, (EXTRA, kv_out.shape[1])
            ).astype(kv_out.dtype)

    return kern


def query_kernel(heads):
    def kern(st, rc, st_own, st_near, st_two, near, two, three, unused, own_out, partner_out):
        for a in range(2):
            for h in range(heads):
                i = a * heads + h
                total = near[i] * ratio_of(st, rc, (st_own, st_near)[a], a, h)
                total = total + two[i] * ratio_of(st, rc, st_two, a, h)
                total = total + three[i] * ratio_of(st, rc, st, a, h)
                if a == 0:
                    own_out[h] = total
                else:
                    partner_out[h] = total.astype(bf16)

    return kern


def comp_kernel(heads, c):
    def kern(q_ref, g_ref, st, rc, kc_ref, vc_ref, dq_in, kv_out, dq_out):
        rows = q_ref.shape[0]
        mask = causal(st[38:39, :], rows)
        k = kc_ref[...]
        v = vc_ref[...]
        kt = jnp.transpose(k)
        kv_out[...] = jnp.zeros_like(kv_out)

        @pl.loop(0, heads)
        def _(h):
            q = head(q_ref, h)
            g = head(g_ref, h, rows)
            lse = lse_of(st, rc, 0, h)
            delta = row(st, 32 + h)
            s = jnp.where(mask, dg(k, q, 1, 1) * c, masked_score)
            p = jnp.exp2(s - lse)
            ds = (p * (dg(v, g, 1, 1) - delta)).astype(bf16)
            kv_out[:, :128] += dg(ds, q, 1, 0)
            kv_out[:, 128:] += dg(p.astype(bf16), g, 1, 0)
            dq_out[h] = dq_in[h] + dg(kt, ds, 1, 0)

    return kern


def up_kernel(n):
    def kern(near, three, up):
        up[...] = (near[2 * n :] + three[2 * n :].astype(f32)).astype(bf16)

    return kern


def down_kernel(n):
    def kern(near, three, two, unused, down, keep):
        down[...] = (near[:n] + three[:n].astype(f32) + two[:n].astype(f32)).astype(bf16)
        keep[...] = near[n : 2 * n] + three[n : 2 * n].astype(f32) + two[n:].astype(f32)

    return kern


def turn_kernel(heads):
    def kern(dq_own, dq_rc, unused, out):
        for h in range(heads):
            out[:, h * 128 : (h + 1) * 128] = jnp.transpose(dq_own[h] + dq_rc[h].astype(f32))

    return kern


def end_kernel(scale, n_keys, all_slots):
    def kern(keep, one_rc, two_rc, ckv, dq_sum, dq, dkc, dvc, dkp, dvp):
        kv = keep[...] + one_rc[...].astype(f32) + two_rc[...].astype(f32)
        factor = (all_slots / (BLOCK * kv[n_keys : n_keys + 1, :]))[:, :128]
        both = factor * scale
        dkp[...] = (kv[:n_keys, :128] * both).astype(bf16)
        dvp[...] = (kv[:n_keys, 128:] * factor).astype(bf16)
        dkc[...] = (ckv[:, :128] * both).astype(bf16)
        dvc[...] = (ckv[:, 128:] * factor).astype(bf16)
        for h in range(dq.shape[1] // 128):
            dq[:, h * 128 : (h + 1) * 128] = (head(dq_sum, h) * both).astype(bf16)

    return kern


def along_z(value, step, n_dp, n_z):
    pairs = []
    for d in range(n_dp):
        turn = step if d % 2 == 0 else -step
        for x in range(2):
            for z in range(n_z):
                source = (d * 2 + x) * n_z + z
                pairs.append((source, (d * 2 + x) * n_z + (z + turn) % n_z))
    return lax.ppermute(value, ("dp", "ctx"), pairs)


def across_x(value, n_z):
    return lax.ppermute(value, "ctx", [(i, (i + n_z) % (2 * n_z)) for i in range(2 * n_z)])


def per_device(
    q_comp, k_comp, v_comp, o_comp, d_out, k_prompt, v_prompt, kept_counts, comp_len, owner_list
):
    n_ctx = lax.axis_size("ctx")
    n_dp = lax.axis_size("dp")
    n_z = n_ctx // 2
    position = lax.axis_index("ctx")
    q, kc, vc = q_comp[0], k_comp[0], v_comp[0]
    o, d, k, v = o_comp[0], d_out[0], k_prompt[0], v_prompt[0]
    rows, width = q.shape
    n_keys, d_head = k.shape
    heads = width // d_head
    scale = d_head ** (-0.5)
    c = scale * LOG2E
    pair_flops = 2 * rows * heads * d_head

    lists = [kept_counts, comp_len, owner_list]

    def zmove(value, step):
        return along_z(value, step, n_dp, n_z)

    def after(value, *others):
        return lax.optimization_barrier((value, *others))[0]

    kv = call(
        pack_kernel,
        [sds((n_keys, 2 * d_head), bf16)],
        [k, v],
        hbm=(0, 1),
        scratch=[pltpu.SemaphoreType.DMA((2,))],
    )[0]
    kv_dn = zmove(kv, 3)
    kv_up = zmove(kv, -3)
    qp = across_x(q, n_z)
    st, cnt, q, kc, d, vc = call(
        first_kernel(heads, c),
        [sds((40, rows)), sds((8, 128))]
        + [sds(x, bf16) for x in (q.shape, kc.shape, (rows + EXTRA, width), vc.shape)],
        [*lists, q, kc, d, o, vc],
        flops=pair_flops * (n_keys + rows) * 2,
        hbm=range(1, 8),
        anywhere=(0,),
        scratch=[pltpu.SMEM(x.shape, jnp.int32) for x in lists]
        + [pltpu.VMEM(o.shape, bf16), pltpu.SemaphoreType.DMA((8,))],
    )

    cnt = lax.ppermute(
        cnt,
        ("dp", "ctx"),
        [(e * n_ctx + x, (e - x) % n_dp * n_ctx + x) for e in range(n_dp) for x in range(n_ctx)],
    )

    def joined(offset, *tokens):
        return call(
            join_kernel(offset, d_head),
            [sds((3 * n_keys, d_head), bf16), sds((2 * n_keys, d_head), bf16)],
            [kv_dn, kv, kv_up, *tokens],
        )

    def stats(q_list, st, k_set, sides, cnt=None):
        return call(
            stat_kernel(heads, c, sides, cnt is not None),
            [sds((40, rows)), sds((heads * len(q_list), k_set.shape[0], rows), bf16)],
            [*q_list, st] + ([] if cnt is None else [cnt]) + [k_set],
            flops=pair_flops * k_set.shape[0] * len(q_list) * 2,
        )

    own, partner = (0, True), (16, True)
    k_near, k_pair = joined(0, st, cnt)
    k_three = zmove(k_near, 1)
    k_two = zmove(k_pair, -1)
    st_own, e_own = stats([q], st, k_near, [own], cnt)
    gp = across_x(after(d, qp, st_own), n_z)
    st_near, e_par = stats([qp], st_own, k_near, [(16, False)])
    v_near, v_pair = joined(d_head, st_near)
    v_three = zmove(v_near, 1)
    v_two = zmove(v_pair, -1)
    st_two, e_two = stats([q, qp], st_near, k_two, [own, partner])
    st, e_three = stats([q, qp], st_two, k_three, [own, partner])
    rc = across_x(st, n_z)

    def early(k_set, v_set, e_sets, token):
        return call(
            early_kernel(heads, len(e_sets) == 2, 1),
            [sds((2 * heads, k_set.shape[0], rows), bf16), sds((2 * heads, d_head, rows))],
            [d, gp, k_set, v_set, *e_sets, token],
        )

    def late(ds, m_own, m_par, e_sets, out_type, token):
        total = ds.shape[1]
        return call(
            late_kernel(heads, n_keys, len(e_sets) == 2, 1),
            [sds((total // n_keys * (n_keys + EXTRA), 2 * d_head), out_type)],
            [q, qp, d, gp, st, rc, m_own, m_par, ds, *e_sets, token],
            scratch=[pltpu.VMEM((total, d_head), f32)] * 2
            + [pltpu.VMEM((2 * heads, rows, d_head), bf16)] * 2,
        )[0]

    ds_three, dq_three = early(k_three, v_three, [e_three], st)
    kv_three = late(ds_three, st, st, [e_three], bf16, v_two)
    in_three = zmove(kv_three, -1)
    ds_two, dq_two = early(k_two, v_two, [e_two], kv_three)
    kv_two = late(ds_two, st_two, st_two, [e_two], bf16, dq_two)
    in_two = zmove(kv_two, 1)
    ds_near, dq_near = early(k_near, v_near, [e_own, e_par], kv_two)
    dq, dqp = call(
        query_kernel(heads),
        [sds((heads, d_head, rows)), sds((heads, d_head, rows), bf16)],
        [st, rc, st_own, st_near, st_two, dq_near, dq_two, dq_three, kv_two],
    )
    dq_rc = across_x(dqp, n_z)
    kv_near = late(ds_near, st_own, st_near, [e_own, e_par], f32, dqp)
    block = (n_keys + EXTRA, 2 * d_head)
    up = call(up_kernel(block[0]), [sds(block, bf16)], [kv_near, in_three])[0]
    from_dn = zmove(up, 3)
    down, keep = call(
        down_kernel(block[0]),
        [sds(block, bf16), sds(block)],
        [kv_near, in_three, in_two, up],
    )
    from_up = zmove(down, -3)
    ckv, dq = call(
        comp_kernel(heads, c),
        [sds((rows, 2 * d_head)), sds((heads, d_head, rows))],
        [q, d, st, rc, kc, vc, dq],
    )
    dq = call(turn_kernel(heads), [sds((rows, width))], [dq, dq_rc, from_dn])[0]
    outs = call(
        end_kernel(scale, n_keys, float(n_dp * n_ctx * rows)),
        [
            sds((rows, width), bf16),
            sds((rows, d_head), bf16),
            sds((rows, d_head), bf16),
            sds((n_keys, d_head), bf16),
            sds((n_keys, d_head), bf16),
        ],
        [keep, from_dn, from_up, ckv, dq],
    )
    return tuple(x[None] for x in outs)


def solution(mesh):
    split = P("dp", "ctx", None)
    return jax.shard_map(
        per_device,
        mesh=mesh,
        in_specs=(split,) * 7 + (P("dp"), P("dp", None), P("dp", None)),
        out_specs=(split,) * 5,
        check_vma=False,
    )
```

```python
import jax
import jax.numpy as jnp
from jax import lax
from jax.experimental import pallas as pl
from jax.experimental.pallas import tpu as pltpu
from jax.sharding import PartitionSpec as P

BLOCK = 128
EXTRA = 16
FAR = 40.0
LOG2E = 1.4426950408889634
masked_score = -1e30
f32 = jnp.float32
bf16 = jnp.bfloat16


def dg(a, b, ca, cb):
    return lax.dot_general(a, b, (((ca,), (cb,)), ((), ())), preferred_element_type=f32)


def call(kern, outs, ins, flops=0, hbm=(), anywhere=(), scratch=(), vmem=16):
    total = sum(x.size * x.dtype.itemsize for x in ins) + sum(
        o.size * o.dtype.itemsize for o in outs
    )
    spaces = {**{i: pltpu.HBM for i in hbm}, **{i: pl.ANY for i in anywhere}}
    specs = [pl.BlockSpec(memory_space=spaces.get(i, pltpu.VMEM)) for i in range(len(ins))]
    ins = [
        pltpu.with_memory_space_constraint(x, pltpu.HBM) if i in hbm else x
        for i, x in enumerate(ins)
    ]
    return pl.pallas_call(
        kern,
        out_shape=outs,
        in_specs=specs,
        out_specs=[pl.BlockSpec(memory_space=pltpu.VMEM)] * len(outs),
        scratch_shapes=list(scratch),
        compiler_params=pltpu.CompilerParams(vmem_limit_bytes=vmem * 2**20),
        cost_estimate=pl.CostEstimate(flops=int(flops), bytes_accessed=1, transcendentals=0),
    )(*ins)


def sds(shape, dtype=f32):
    return jax.ShapeDtypeStruct(shape, dtype)


def head(ref, h, rows=None):
    if isinstance(h, int):
        return ref[:rows, h * 128 : (h + 1) * 128]
    return ref[:rows, pl.ds(pl.multiple_of(h * 128, 128), 128)]


def row(ref, i):
    return ref[pl.ds(i, 1), :]


def delta_of(ref, rows, h):
    parts = ref[rows : rows + EXTRA, :rows].astype(f32)
    return parts[3 * h : 3 * h + 1] + parts[3 * h + 1 : 3 * h + 2] + parts[3 * h + 2 : 3 * h + 3]


def run_info(kept, lens, owners, position):
    blocks = same = used = jnp.int32(0)
    for j in range(lens.shape[1]):
        n = jnp.where(j < kept[0], lens[0, j], 0)
        mine = jnp.where(owners[0, j] == position, n, 0)
        used = used + n
        blocks = blocks + mine
        same = jnp.maximum(same, mine - 1)
    return blocks, same, used


def causal(same, n):
    key = lax.broadcasted_iota(jnp.int32, (n, n), 0)
    row = lax.broadcasted_iota(jnp.int32, (n, n), 1)
    same_block = (key // BLOCK) == (row // BLOCK)
    return (key <= row) & (same_block | (same > 0))


def pack_kernel(k_any, v_any, kv_ref, sems):
    width = k_any.shape[1]
    one = pltpu.make_async_copy(k_any, kv_ref.at[:, :width], sems.at[0])
    two = pltpu.make_async_copy(v_any, kv_ref.at[:, width:], sems.at[1])
    one.start()
    two.start()
    one.wait()
    two.wait()


def first_kernel(heads, c):
    def kern(
        kept_any, lens_any, owners_any, q_any, kc_any, d_any, o_any, vc_any,
        st_ref, cnt_ref, q_ref, kc_ref, d_ref, vc_ref,
        kept, lens, owners, o_ref, sems,
    ):
        pairs = (
            (kept_any, kept), (lens_any, lens), (owners_any, owners),
            (q_any, q_ref), (kc_any, kc_ref), (d_any, d_ref.at[pl.ds(0, q_any.shape[0]), :]),
            (o_any, o_ref),
            (vc_any, vc_ref),
        )
        copies = [pltpu.make_async_copy(x, y, sems.at[i]) for i, (x, y) in enumerate(pairs)]
        for copy in copies:
            copy.start()
        for copy in copies[:3]:
            copy.wait()
        rows = q_ref.shape[0]
        blocks, same, used = run_info(kept, lens, owners, lax.axis_index("ctx"))
        empty = lax.broadcasted_iota(jnp.int32, (1, rows), 1) // BLOCK >= blocks
        mask = causal(same, rows)
        st_ref[...] = jnp.zeros_like(st_ref)
        cnt_ref[...] = jnp.full(cnt_ref.shape, used.astype(f32))
        st_ref[38:39, :] = jnp.full((1, rows), same.astype(f32))
        for copy in copies[3:5]:
            copy.wait()
        kc = kc_ref[...]
        for h in range(heads):
            q = head(q_ref, h)
            comp = jnp.where(mask, dg(kc, q, 1, 1) * c, masked_score)
            top = jnp.max(comp, axis=0, keepdims=True)
            total = jnp.sum(jnp.exp2(comp - top), axis=0, keepdims=True)
            st_ref[h : h + 1, :] = jnp.where(empty, -masked_score, top)
            st_ref[8 + h : 9 + h, :] = jnp.where(empty, 1.0, total)
        for copy in copies[5:]:
            copy.wait()
        parts = []
        for h in range(heads):
            prod = head(d_ref, h, rows).astype(f32) * head(o_ref, h).astype(f32)
            delta = jnp.sum(jnp.transpose(prod), axis=0, keepdims=True)
            st_ref[32 + h : 33 + h, :] = delta
            high = delta.astype(bf16).astype(f32)
            mid = (delta - high).astype(bf16).astype(f32)
            parts += [high, mid, delta - high - mid]
        parts.append(jnp.zeros((EXTRA - len(parts), rows), f32))
        d_ref[rows : rows + EXTRA, :] = jnp.zeros((EXTRA, d_ref.shape[1]), bf16)
        d_ref[rows : rows + EXTRA, :rows] = jnp.concatenate(parts, axis=0).astype(bf16)

    return kern


def stat_kernel(heads, c, sides, counted=False):
    def kern(*refs):
        q_refs, refs = refs[: len(sides)], refs[len(sides) :]
        st_in, refs = refs[0], refs[1:]
        if counted:
            cnt, refs = refs[0], refs[1:]
        k_ref, st_ref, e_ref = refs
        st_ref[...] = st_in[...]
        if counted:
            st_ref[37:38, :] = jnp.concatenate([cnt[0:1, :]] * (st_ref.shape[1] // 128), axis=1)

        def score(a, h):
            return dg(k_ref[...], head(q_refs[a], h), 1, 1) * c

        def rows_of(a, h):
            base = sides[a][0]
            return pl.ds(base + h, 1), pl.ds(base + 8 + h, 1)

        def exact(a, h, source):
            m_row, l_row = rows_of(a, h)
            scores = score(a, h)
            top = jnp.max(scores, axis=0, keepdims=True)
            if sides[a][1]:
                m_old = source[m_row, :]
                top = jnp.maximum(top, m_old)
            e = jnp.exp2(scores - top)
            total = jnp.sum(e, axis=0, keepdims=True)
            if sides[a][1]:
                total = total + source[l_row, :] * jnp.exp2(m_old - top)
            e_ref[a * heads + h] = e.astype(bf16)
            st_ref[m_row, :] = top
            st_ref[l_row, :] = total

        worst = None
        for a in range(len(sides)):
            for h in range(heads):
                m_row, l_row = rows_of(a, h)
                above = score(a, h) - st_in[m_row, :]
                e = jnp.exp2(above)
                e_ref[a * heads + h] = e.astype(bf16)
                st_ref[l_row, :] = st_in[l_row, :] + jnp.sum(e, axis=0, keepdims=True)
                high = jnp.max(above, axis=0, keepdims=True)
                if not sides[a][1]:
                    high = jnp.abs(high)
                worst = high if worst is None else jnp.maximum(worst, high)

        @pl.when(jnp.max(worst) > FAR)
        def _():
            for a in range(len(sides)):

                @pl.loop(0, heads)
                def _(h):
                    exact(a, h, st_in)

    return kern


def join_kernel(offset, width):
    def kern(dn, own, up, *rest):
        near, pair = rest[-2:]
        n = own.shape[0]
        for i, ref in enumerate((dn, own, up)):
            part = ref[:, offset : offset + width]
            near[i * n : (i + 1) * n, :] = part
            if i < 2:
                pair[i * n : (i + 1) * n, :] = part

    return kern


def merged_lse(m_one, l_one, m_two, l_two):
    top = jnp.maximum(m_one, m_two)
    return top + jnp.log2(l_one * jnp.exp2(m_one - top) + l_two * jnp.exp2(m_two - top))


def lse_of(st, rc, a, h):
    b = 16 - 16 * a
    o = 16 * a
    return merged_lse(row(st, o + h), row(st, o + 8 + h), row(rc, b + h), row(rc, b + 8 + h))


def early_kernel(heads, split, n_tokens):
    def kern(go, gp, k_ref, v_ref, *refs):
        e_refs, (ds_out, dq_out) = refs[: 1 + split], refs[1 + split + n_tokens :]
        rows = e_refs[0].shape[2]
        v = v_ref[...]
        kt = jnp.transpose(k_ref[...])
        for a in range(2):
            for h in range(heads):
                i = a * heads + h
                g = head((go, gp)[a], h, rows)
                delta = delta_of((go, gp)[a], rows, h)
                e = e_refs[a][h] if split else e_refs[0][i]
                ds_out[i] = (e.astype(f32) * (dg(v, g, 1, 1) - delta)).astype(bf16)
        for i in range(2 * heads):
            dq_out[i] = dg(kt, ds_out[i], 1, 0)

    return kern


def ratio_of(st, rc, top, a, h):
    i = 16 * a + h
    return jnp.exp2(top[i : i + 1, :] - lse_of(st, rc, a, h))


def late_kernel(heads, n_keys, split, n_tokens):
    def kern(qo, qp, go, gp, st, rc, mo, mp, ds_ref, *refs):
        e_refs, (kv_out, dk_s, dv_s, q_s, g_s) = refs[: 1 + split], refs[1 + split + n_tokens :]
        rows = qo.shape[0]
        for a in range(2):
            for h in range(heads):
                i = a * heads + h
                ratio = ratio_of(st, rc, (mo, mp)[a], a, h)
                column = jnp.transpose(jnp.broadcast_to(ratio, (128, rows)))
                q_s[i] = (head((qo, qp)[a], h).astype(f32) * column).astype(bf16)
                g_s[i] = (head((go, gp)[a], h, rows).astype(f32) * column).astype(bf16)
        for a in range(2):
            for h in range(heads):
                i = a * heads + h
                e = e_refs[a][h] if split else e_refs[0][i]
                dv = dg(e, g_s[i], 1, 0)
                dk = dg(ds_ref[i], q_s[i], 1, 0)
                if i == 0:
                    dk_s[...] = dk
                    dv_s[...] = dv
                else:
                    dk_s[...] += dk
                    dv_s[...] += dv
        count = st[37:38, :] + rc[37:38, :]
        step = n_keys + EXTRA
        for b in range(ds_ref.shape[1] // n_keys):
            part = pl.ds(b * n_keys, n_keys)
            kv_out[b * step : b * step + n_keys, :128] = dk_s[part, :].astype(kv_out.dtype)
            kv_out[b * step : b * step + n_keys, 128:] = dv_s[part, :].astype(kv_out.dtype)
            kv_out[b * step + n_keys : (b + 1) * step, :] = jnp.broadcast_to(
                count, (EXTRA, kv_out.shape[1])
            ).astype(kv_out.dtype)

    return kern


def query_kernel(heads):
    def kern(st, rc, st_own, st_near, st_two, near, two, three, unused, own_out, partner_out):
        for a in range(2):
            for h in range(heads):
                i = a * heads + h
                total = near[i] * ratio_of(st, rc, (st_own, st_near)[a], a, h)
                total = total + two[i] * ratio_of(st, rc, st_two, a, h)
                total = total + three[i] * ratio_of(st, rc, st, a, h)
                if a == 0:
                    own_out[h] = total
                else:
                    partner_out[h] = total.astype(bf16)

    return kern


def comp_kernel(heads, c):
    def kern(q_ref, g_ref, st, rc, kc_ref, vc_ref, dq_in, kv_out, dq_out):
        rows = q_ref.shape[0]
        mask = causal(st[38:39, :], rows)
        k = kc_ref[...]
        v = vc_ref[...]
        kt = jnp.transpose(k)
        kv_out[...] = jnp.zeros_like(kv_out)

        @pl.loop(0, heads)
        def _(h):
            q = head(q_ref, h)
            g = head(g_ref, h, rows)
            lse = lse_of(st, rc, 0, h)
            delta = row(st, 32 + h)
            s = jnp.where(mask, dg(k, q, 1, 1) * c, masked_score)
            p = jnp.exp2(s - lse)
            ds = (p * (dg(v, g, 1, 1) - delta)).astype(bf16)
            kv_out[:, :128] += dg(ds, q, 1, 0)
            kv_out[:, 128:] += dg(p.astype(bf16), g, 1, 0)
            dq_out[h] = dq_in[h] + dg(kt, ds, 1, 0)

    return kern


def up_kernel(n):
    def kern(near, three, up):
        up[...] = (near[2 * n :] + three[2 * n :].astype(f32)).astype(bf16)

    return kern


def down_kernel(n):
    def kern(near, three, two, unused, down, keep):
        down[...] = (near[:n] + three[:n].astype(f32) + two[:n].astype(f32)).astype(bf16)
        keep[...] = near[n : 2 * n] + three[n : 2 * n].astype(f32) + two[n:].astype(f32)

    return kern


def turn_kernel(heads):
    def kern(dq_own, dq_rc, unused, out):
        for h in range(heads):
            out[:, h * 128 : (h + 1) * 128] = jnp.transpose(dq_own[h] + dq_rc[h].astype(f32))

    return kern


def end_kernel(scale, n_keys, all_slots):
    def kern(keep, one_rc, two_rc, ckv, dq_sum, dq, dkc, dvc, dkp, dvp):
        kv = keep[...] + one_rc[...].astype(f32) + two_rc[...].astype(f32)
        factor = (all_slots / (BLOCK * kv[n_keys : n_keys + 1, :]))[:, :128]
        both = factor * scale
        dkp[...] = (kv[:n_keys, :128] * both).astype(bf16)
        dvp[...] = (kv[:n_keys, 128:] * factor).astype(bf16)
        dkc[...] = (ckv[:, :128] * both).astype(bf16)
        dvc[...] = (ckv[:, 128:] * factor).astype(bf16)
        for h in range(dq.shape[1] // 128):
            dq[:, h * 128 : (h + 1) * 128] = (head(dq_sum, h) * both).astype(bf16)

    return kern


def along_z(value, step, n_dp, n_z):
    pairs = []
    for d in range(n_dp):
        turn = step if d % 2 == 0 else -step
        for x in range(2):
            for z in range(n_z):
                source = (d * 2 + x) * n_z + z
                pairs.append((source, (d * 2 + x) * n_z + (z + turn) % n_z))
    return lax.ppermute(value, ("dp", "ctx"), pairs)


def across_x(value, n_z):
    return lax.ppermute(value, "ctx", [(i, (i + n_z) % (2 * n_z)) for i in range(2 * n_z)])


def per_device(
    q_comp, k_comp, v_comp, o_comp, d_out, k_prompt, v_prompt, kept_counts, comp_len, owner_list
):
    n_ctx = lax.axis_size("ctx")
    n_dp = lax.axis_size("dp")
    n_z = n_ctx // 2
    position = lax.axis_index("ctx")
    q, kc, vc = q_comp[0], k_comp[0], v_comp[0]
    o, d, k, v = o_comp[0], d_out[0], k_prompt[0], v_prompt[0]
    rows, width = q.shape
    n_keys, d_head = k.shape
    heads = width // d_head
    scale = d_head ** (-0.5)
    c = scale * LOG2E
    pair_flops = 2 * rows * heads * d_head

    lists = [kept_counts, comp_len, owner_list]

    def zmove(value, step):
        return along_z(value, step, n_dp, n_z)

    def after(value, *others):
        return lax.optimization_barrier((value, *others))[0]

    kv = call(
        pack_kernel,
        [sds((n_keys, 2 * d_head), bf16)],
        [k, v],
        hbm=(0, 1),
        scratch=[pltpu.SemaphoreType.DMA((2,))],
    )[0]
    kv_dn = zmove(kv, 3)
    kv_up = zmove(kv, -3)
    qp = across_x(q, n_z)
    st, cnt, q, kc, d, vc = call(
        first_kernel(heads, c),
        [sds((40, rows)), sds((8, 128))]
        + [sds(x, bf16) for x in (q.shape, kc.shape, (rows + EXTRA, width), vc.shape)],
        [*lists, q, kc, d, o, vc],
        flops=pair_flops * (n_keys + rows) * 2,
        hbm=range(1, 8),
        anywhere=(0,),
        scratch=[pltpu.SMEM(x.shape, jnp.int32) for x in lists]
        + [pltpu.VMEM(o.shape, bf16), pltpu.SemaphoreType.DMA((8,))],
    )

    cnt = lax.ppermute(
        cnt,
        ("dp", "ctx"),
        [(e * n_ctx + x, (e - x) % n_dp * n_ctx + x) for e in range(n_dp) for x in range(n_ctx)],
    )

    def joined(offset, *tokens):
        return call(
            join_kernel(offset, d_head),
            [sds((3 * n_keys, d_head), bf16), sds((2 * n_keys, d_head), bf16)],
            [kv_dn, kv, kv_up, *tokens],
        )

    def stats(q_list, st, k_set, sides, cnt=None):
        return call(
            stat_kernel(heads, c, sides, cnt is not None),
            [sds((40, rows)), sds((heads * len(q_list), k_set.shape[0], rows), bf16)],
            [*q_list, st] + ([] if cnt is None else [cnt]) + [k_set],
            flops=pair_flops * k_set.shape[0] * len(q_list) * 2,
        )

    own, partner = (0, True), (16, True)
    k_near, k_pair = joined(0, st, cnt)
    k_three = zmove(k_near, 1)
    k_two = zmove(k_pair, -1)
    st_own, e_own = stats([q], st, k_near, [own], cnt)
    gp = across_x(after(d, qp, st_own), n_z)
    st_near, e_par = stats([qp], st_own, k_near, [(16, False)])
    v_near, v_pair = joined(d_head, st_near)
    v_three = zmove(v_near, 1)
    v_two = zmove(v_pair, -1)
    st_two, e_two = stats([q, qp], st_near, k_two, [own, partner])
    st, e_three = stats([q, qp], st_two, k_three, [own, partner])
    rc = across_x(st, n_z)

    def early(k_set, v_set, e_sets, token):
        return call(
            early_kernel(heads, len(e_sets) == 2, 1),
            [sds((2 * heads, k_set.shape[0], rows), bf16), sds((2 * heads, d_head, rows))],
            [d, gp, k_set, v_set, *e_sets, token],
        )

    def late(ds, m_own, m_par, e_sets, out_type, token):
        total = ds.shape[1]
        return call(
            late_kernel(heads, n_keys, len(e_sets) == 2, 1),
            [sds((total // n_keys * (n_keys + EXTRA), 2 * d_head), out_type)],
            [q, qp, d, gp, st, rc, m_own, m_par, ds, *e_sets, token],
            scratch=[pltpu.VMEM((total, d_head), f32)] * 2
            + [pltpu.VMEM((2 * heads, rows, d_head), bf16)] * 2,
        )[0]

    ds_three, dq_three = early(k_three, v_three, [e_three], st)
    kv_three = late(ds_three, st, st, [e_three], bf16, v_two)
    in_three = zmove(kv_three, -1)
    ds_two, dq_two = early(k_two, v_two, [e_two], kv_three)
    kv_two = late(ds_two, st_two, st_two, [e_two], bf16, dq_two)
    in_two = zmove(kv_two, 1)
    ds_near, dq_near = early(k_near, v_near, [e_own, e_par], kv_two)
    dq, dqp = call(
        query_kernel(heads),
        [sds((heads, d_head, rows)), sds((heads, d_head, rows), bf16)],
        [st, rc, st_own, st_near, st_two, dq_near, dq_two, dq_three, kv_two],
    )
    dq_rc = across_x(dqp, n_z)
    kv_near = late(ds_near, st_own, st_near, [e_own, e_par], f32, dqp)
    block = (n_keys + EXTRA, 2 * d_head)
    up = call(up_kernel(block[0]), [sds(block, bf16)], [kv_near, in_three])[0]
    from_dn = zmove(up, 3)
    down, keep = call(
        down_kernel(block[0]),
        [sds(block, bf16), sds(block)],
        [kv_near, in_three, in_two, up],
    )
    from_up = zmove(down, -3)
    ckv, dq = call(
        comp_kernel(heads, c),
        [sds((rows, 2 * d_head)), sds((heads, d_head, rows))],
        [q, d, st, rc, kc, vc, dq],
    )
    dq = call(turn_kernel(heads), [sds((rows, width))], [dq, dq_rc, from_dn])[0]
    outs = call(
        end_kernel(scale, n_keys, float(n_dp * n_ctx * rows)),
        [
            sds((rows, width), bf16),
            sds((rows, d_head), bf16),
            sds((rows, d_head), bf16),
            sds((n_keys, d_head), bf16),
            sds((n_keys, d_head), bf16),
        ],
        [keep, from_dn, from_up, ckv, dq],
    )
    return tuple(x[None] for x in outs)


def solution(mesh):
    split = P("dp", "ctx", None)
    return jax.shard_map(
        per_device,
        mesh=mesh,
        in_specs=(split,) * 7 + (P("dp"), P("dp", None), P("dp", None)),
        out_specs=(split,) * 5,
        check_vma=False,
    )
```
